256 devices in a mesh: seq: 64 (over z, x_hi, y), head: 4 (over x_lo, core).
Axes of the slice: x: 4 (x_hi: 2, x_lo: 2; x = x_hi * 2 + x_lo), y: 4, z: 8, core: 2. Of those that a mesh axis runs over, the one named last changes fastest.
Arguments:
- hidden_in: bfloat16 [5120, 7168], P('seq', 'head'), may hold values from -6 to 6
- w_down: bfloat16 [7168, 576], P('head'), may hold values from -0.0625 to 0.0625
- kv_gain: bfloat16 [512], replicated, may hold values from 0.099609375 to 1.8984375
- queries: bfloat16 [5120, 12288], P('seq', 'head'), may hold values from -140 to 140
- w_key: bfloat16 [512, 8192], P(None, 'head'), may hold values from -0.25 to 0.25
- w_value: bfloat16 [512, 8192], P(None, 'head'), may hold values from -1.25 to 1.25
Outputs:
- values_out: bfloat16 [5120, 8192], P('seq', 'head')
The draws below stay inside these ranges and needn't reach their ends.
All inputs are finite; a program needn't handle non-finite values.
Results may differ from the reference program's by a relative error of at most 0.013.
The reference program's roundings to bfloat16 on the way (of `latent`, `key_rope`, `query_rope`, `query_latent` and `attended`) count: a program that leaves them out, or rounds other values in their place, can miss the bound.
Values may be sent and summed in bfloat16 or wider, within the bound.
A program may use at most 128 MiB of HBM per device.

```python
import jax
import jax.numpy as jnp
from jax import lax

D = 7168
LAT = 512
ROPE = 64
NOPE = 128
VDIM = 128
H = 64
TOK_DEV = 80
TOKENS = 5120
N_SEQ = 64


def draw_queries(key, part):
    key = jax.random.fold_in(key, 11)
    base_key = jax.random.fold_in(key, 0)
    shape = (TOKENS, H * (NOPE + ROPE))
    return (jax.random.truncated_normal(base_key, -6.0, 6.0, shape, jnp.float32) * 2.0).astype(jnp.bfloat16)


def shard_levels(rng, dims, cuts, smallest, high):
    level = 1.0
    for position, parts in cuts:
        heights = jax.random.uniform(jax.random.fold_in(jax.random.fold_in(rng, 6), position), (parts,), jnp.float32, smallest / len(cuts), high / len(cuts))
        level = level * jnp.repeat(jnp.exp(heights), dims[position] // parts).reshape((-1,) + (1,) * (len(dims) - 1 - position))
    return level


def normal_values(rng, shape, spread, limit, pieces=(), held_as=jnp.bfloat16):
    entries = spread * jax.random.normal(rng, shape, jnp.float32)
    if pieces:
        entries = entries * shard_levels(rng, shape, pieces, -0.22, 0.18)
    return jnp.clip(entries, -limit, limit).astype(held_as)


def setup_inputs(seed: int = 0) -> dict:
    splits = jax.random.split(jax.random.key(seed), 7)
    hidden_in = normal_values(splits[0], (TOKENS, D), 1.0, 6.0, ((0, 64), (1, 4)))
    w_down = normal_values(splits[1], (D, LAT + ROPE), D ** -0.5, 0.0625, ((0, 4),))
    kv_gain = jnp.clip(1.0 + 0.18 * jax.random.normal(splits[2], (LAT,), jnp.float32), 0.099609375, 1.8984375).astype(jnp.bfloat16)
    queries = draw_queries(jax.random.fold_in(splits[6], 71), 0)
    w_key = normal_values(splits[4], (LAT, H * NOPE), LAT ** -0.5, 0.25, ((1, 4),))
    w_value = normal_values(splits[5], (LAT, H * VDIM), (max(LAT // 25, 1)) ** -0.5, 1.25, ((1, 4),))
    return dict(hidden_in=hidden_in, w_down=w_down, kv_gain=kv_gain, queries=queries, w_key=w_key, w_value=w_value)


def fold_order(indices, per_device, devices):
    half_rows = per_device // 2
    device = indices // per_device
    offset_in = indices % per_device
    early = device * half_rows + offset_in
    late = (2 * devices - 1 - device) * half_rows + offset_in - half_rows
    return jnp.where(offset_in < half_rows, early, late).astype(jnp.int32)

def rotate(vectors, positions):
    width = vectors.shape[-1] // 2
    inverse = 10000.0 ** (-jnp.arange(width, dtype=jnp.float32) / width)
    angles = positions.astype(jnp.float32)[..., None] * inverse
    cosine = jnp.cos(angles)
    sine = jnp.sin(angles)
    leading = vectors[..., :width]
    trailing = vectors[..., width:]
    return jnp.concatenate([leading * cosine - trailing * sine, trailing * cosine + leading * sine], -1)

def reference(hidden_in, w_down, kv_gain, queries, w_key, w_value):
    positions = fold_order(jnp.arange(TOKENS, dtype=jnp.int32), TOK_DEV, N_SEQ)
    projected = jnp.dot(hidden_in, w_down, preferred_element_type=jnp.float32)
    raw_latent = projected[:, :LAT]
    mean_square = lax.optimization_barrier(jnp.mean(raw_latent * raw_latent, axis=1, keepdims=True))
    latent = (raw_latent * lax.rsqrt(mean_square + 1e-06) * kv_gain.astype(jnp.float32)).astype(jnp.bfloat16)
    key_rope = rotate(projected[:, LAT:], positions).astype(jnp.bfloat16)
    scale_factor = (NOPE + ROPE) ** (-0.5)
    shaped = queries.astype(jnp.float32).reshape(TOKENS, H, NOPE + ROPE)
    query_rope = (rotate(shaped[:, :, NOPE:], positions[:, None]) * scale_factor).astype(jnp.bfloat16)
    key_weight = w_key.astype(jnp.float32).reshape(LAT, H, NOPE)
    query_latent = (jnp.einsum('thd,chd->thc', shaped[:, :, :NOPE], key_weight) * scale_factor).astype(jnp.bfloat16)
    value_weight = w_value.reshape(LAT, H, VDIM).transpose(1, 0, 2)
    allowed = positions[None, :] <= positions[:, None]

    def one_head(items):
        head_latent, head_rope, head_value = items
        scores = jnp.dot(head_latent, latent.T, preferred_element_type=jnp.float32)
        scores = scores + jnp.dot(head_rope, key_rope.T, preferred_element_type=jnp.float32)
        scores = jnp.where(allowed, scores, -1e+30)
        highest = lax.optimization_barrier(jnp.max(scores, axis=1, keepdims=True))
        weights = jnp.where(allowed, jnp.exp(scores - highest), 0.0)
        total = lax.optimization_barrier(jnp.sum(weights, axis=1, keepdims=True))
        attended = (jnp.dot(weights.astype(jnp.bfloat16), latent, preferred_element_type=jnp.float32) / total).astype(jnp.bfloat16)
        return jnp.dot(attended, head_value, preferred_element_type=jnp.float32).astype(jnp.bfloat16)
    per_head = lax.map(one_head, (query_latent.transpose(1, 0, 2), query_rope.transpose(1, 0, 2), value_weight))
    return per_head.transpose(1, 0, 2).reshape(TOKENS, H * VDIM)
```

```python
import functools

import jax
import jax.numpy as jnp
import numpy as np
from jax import lax
from jax.experimental import pallas as pl
from jax.experimental.pallas import tpu as pltpu
from jax.sharding import PartitionSpec as P

F32 = jnp.float32
BF16 = jnp.bfloat16
MESH = pl.DeviceIdType.MESH
LAT, ROPE, NOPE, VDIM = 512, 64, 128, 128
TOK, HALF, HEADS = 80, 40, 16
ROWS = HALF * HEADS
EARLY = 2560
STEP = 512
NT = (((1,), (1,)), ((), ()))
SCALE = (NOPE + ROPE) ** (-0.5)
N_SEMS = 160


def wrap(value, size):
    return lax.rem(value + 2 * size, size)


def place():
    s = lax.axis_index("seq")
    h = lax.axis_index("head")
    x = lax.rem(lax.div(s, 4), 2) * 2 + lax.div(h, 2)
    return x, lax.rem(s, 4), lax.div(s, 8), lax.rem(h, 2)


def device(x, y, z, c):
    x, y, z = wrap(x, 4), wrap(y, 4), wrap(z, 8)
    return (z * 8 + lax.div(x, 2) * 4 + y, lax.rem(x, 2) * 2 + c)


class Comm:
    def __init__(self, send_sems, recv_sems):
        self.send_sems, self.recv_sems = send_sems, recv_sems
        self.sent, self.names = [], {}

    def copy(self, name, src, dst, to):
        i = self.names.setdefault(name, len(self.names))
        return pltpu.make_async_remote_copy(
            src, dst, self.send_sems.at[i], self.recv_sems.at[i], device_id=to, device_id_type=MESH
        )

    def send(self, name, src, to, dst=None):
        copy = self.copy(name, src, src if dst is None else dst, to)
        copy.start()
        self.sent.append(copy)

    def recv(self, name, ref):
        self.copy(name, ref, ref, device(*place())).wait_recv()

    def drain(self):
        for copy in self.sent:
            copy.wait_send()
        self.sent = []


PLANE = [(dx, dy) for dx in range(4) for dy in range(4) if dx or dy]


def greet():
    x, y, z, c = place()
    bar = pltpu.get_barrier_semaphore()
    for dz in range(1, 8):
        pl.semaphore_signal(bar, 1, device_id=device(x, y, z + dz, c), device_id_type=MESH)
    for dx, dy in PLANE:
        pl.semaphore_signal(bar, 1, device_id=device(x + dx, y + dy, z, c), device_id_type=MESH)
    pl.semaphore_signal(bar, 1, device_id=device(x, y, z, 1 - c), device_id_type=MESH)


def meet():
    pl.semaphore_wait(pltpu.get_barrier_semaphore(), 7 + len(PLANE) + 1)


def gather_first(cm, KA, KB, KC):
    x, y, z, c = place()
    for dz in (4, 3, 5, 2, 6, 1, 7):
        cm.send(f"az{dz}", KA.at[c, y, x, z], device(x, y, z + dz, c))
        cm.send(f"bz{dz}", KB.at[c, x, y, z], device(x, y, z + dz, c))
    order = sorted(PLANE, key=lambda t: -(min(t[0], 4 - t[0]) + min(t[1], 4 - t[1])))
    for dx, dy in order:
        cm.send(f"cp{dx}{dy}", KC.at[c, z, x, y], device(x + dx, y + dy, z, c))


def gather_rest(cm, KA, KB, KC):
    x, y, z, c = place()
    sibling = device(x, y, z, 1 - c)

    def X(d):
        return wrap(x + d, 4)

    def Y(d):
        return wrap(y + d, 4)

    def Z(d):
        return wrap(z + d, 8)

    def share(name, ref):
        cm.send("s" + name, ref, sibling)

    for dz in range(1, 8):
        cm.recv(f"az{dz}", KA.at[c, y, x, Z(-dz)])
    for d in (1, -1):
        cm.send(f"ax{d}", KA.at[c, y, x], device(x + d, y, z, c))
    for d in (1, -1):
        cm.send(f"ay{d}_0", KA.at[c, y, x], device(x, y + d, z, c))
    cm.send("ax2", KA.at[c, y, x], device(x + 2, y, z, c))
    share("a00", KA.at[c, y, x])
    for dz in range(1, 8):
        cm.recv(f"bz{dz}", KB.at[c, x, y, Z(-dz)])
    for d in (1, -1):
        cm.send(f"by{d}", KB.at[c, x, y], device(x, y + d, z, c))
    for d in (1, -1):
        cm.send(f"bx{d}_0", KB.at[c, x, y], device(x + d, y, z, c))
    cm.send("by2", KB.at[c, x, y], device(x, y + 2, z, c))
    share("b00", KB.at[c, x, y])
    for dx, dy in PLANE:
        cm.recv(f"cp{dx}{dy}", KC.at[c, z, X(-dx), Y(-dy)])
    for d in (1, -1):
        cm.send(f"cz{d}_1", KC.at[c, z], device(x, y, z + d, c))
    share("c0", KC.at[c, z])
    for d in (1, -1):
        cm.recv(f"ax{d}", KA.at[c, y, X(-d)])
        for e in (1, -1):
            cm.send(f"ay{e}_{-d}", KA.at[c, y, X(-d)], device(x, y + e, z, c))
        share(f"a0{-d}", KA.at[c, y, X(-d)])
        cm.recv(f"by{d}", KB.at[c, x, Y(-d)])
        for e in (1, -1):
            cm.send(f"bx{e}_{-d}", KB.at[c, x, Y(-d)], device(x + e, y, z, c))
        share(f"b0{-d}", KB.at[c, x, Y(-d)])

    def pass_a(e, col):
        cm.recv(f"ay{e}_{col}", KA.at[c, Y(-e), X(col)])
        if (e == 1) == (col in (0, 1)):
            cm.send(f"af_{col}", KA.at[c, Y(-e), X(col)], device(x, y + e, z, c))

    def pass_b(e, col):
        cm.recv(f"bx{e}_{col}", KB.at[c, X(-e), Y(col)])
        if (e == 1) == (col in (0, 1)):
            cm.send(f"bf_{col}", KB.at[c, X(-e), Y(col)], device(x + e, y, z, c))

    def pass_c(k):
        for d in (1, -1):
            cm.recv(f"cz{d}_{k}", KC.at[c, Z(-d * k)])
            if k < 3:
                cm.send(f"cz{d}_{k + 1}", KC.at[c, Z(-d * k)], device(x, y, z + d, c))
            else:
                part = slice(0, 2) if d == 1 else slice(2, 4)
                cm.send(f"cz{d}_4", KC.at[c, Z(-d * k), part], device(x, y, z + d, c))
            share(f"cs{d}{k}", KC.at[c, Z(-d * k)])

    pass_a(1, 0)
    pass_b(1, 0)
    pass_c(1)
    cm.recv("ax2", KA.at[c, y, X(2)])
    for e in (1, -1):
        cm.send(f"ay{e}_2", KA.at[c, y, X(2)], device(x, y + e, z, c))
    share("a02", KA.at[c, y, X(2)])
    cm.recv("by2", KB.at[c, x, Y(2)])
    for e in (1, -1):
        cm.send(f"bx{e}_2", KB.at[c, x, Y(2)], device(x + e, y, z, c))
    share("b02", KB.at[c, x, Y(2)])
    for e, col in ((1, 1), (-1, -1)):
        pass_a(e, col)
        pass_b(e, col)
    pass_c(2)
    for e, col in ((-1, 2), (-1, 0), (1, -1), (-1, 1), (1, 2)):
        pass_a(e, col)
        pass_b(e, col)
    for d in (1, -1):
        share(f"a{d}", KA.at[c, Y(d)])
        share(f"b{d}", KB.at[c, X(d)])
    pass_c(3)
    for col in (0, 1, -1, 2):
        cm.recv(f"af_{col}", KA.at[c, Y(2), X(col)])
        cm.recv(f"bf_{col}", KB.at[c, X(2), Y(col)])
    share("a2", KA.at[c, Y(2)])
    share("b2", KB.at[c, X(2)])
    cm.recv("cz1_4", KC.at[c, Z(4), 0:2])
    cm.recv("cz-1_4", KC.at[c, Z(4), 2:4])
    share("c4", KC.at[c, Z(4)])
    o = 1 - c
    for d in (0, 1, -1, 2):
        cm.recv(f"sa0{d}", KA.at[o, y, X(d)])
        cm.recv(f"sb0{d}", KB.at[o, x, Y(d)])
    for d in (1, -1, 2):
        cm.recv(f"sa{d}", KA.at[o, Y(d)])
        cm.recv(f"sb{d}", KB.at[o, X(d)])
    cm.recv("sc0", KC.at[o, z])
    for k in (1, 2, 3):
        for d in (1, -1):
            cm.recv(f"scs{d}{k}", KC.at[o, Z(-d * k)])
    cm.recv("sc4", KC.at[o, Z(4)])


def lanes(shape):
    return lax.broadcasted_iota(jnp.int32, shape, 1)


def rotated(v, cos, sin):
    width = v.shape[1]
    first = (lanes(v.shape) & 63) < 32
    other = jnp.where(first, pltpu.roll(v, width - 32, 1), pltpu.roll(v, 32, 1))
    return v * cos + other * sin


def fifth(value):
    return (value * 205) >> 10


def body(
    hidden_hbm, down_hbm, gain_ref, inv_ref, queries_hbm, wkey_hbm, wvalue_hbm, out_ref,
    hidden, down, queries, wkey, wvalue, part, got1, mine, got2, KA, KB, KC,
    keys, q, kpos, qpos, cos, sin, scores, top, total, acc,
    load_sems, send_sems, recv_sems,
):
    x, y, z, c = place()
    seq = lax.axis_index("seq")
    x_lo = lax.rem(x, 2)
    loads = [
        pltpu.make_async_copy(src, dst, load_sems.at[i])
        for i, (src, dst) in enumerate(
            (
                (hidden_hbm, hidden),
                (down_hbm, down),
                (queries_hbm, queries),
                (wkey_hbm, wkey),
                (wvalue_hbm, wvalue),
            )
        )
    ]
    for load in loads:
        load.start()
    greet()
    cm = Comm(send_sems, recv_sems)

    token = lax.broadcasted_iota(jnp.int32, (TOK, 128), 0)
    lane = lanes((TOK, 128))
    early_pos = seq * HALF
    late_pos = (127 - seq) * HALF
    position = jnp.where(token < HALF, early_pos + token, late_pos + token - HALF)
    angle = position.astype(F32) * inv_ref[...]
    cos[...] = jnp.cos(angle)
    sine = jnp.sin(angle)
    sin[...] = jnp.where((lane & 63) < 32, -sine, sine)

    e = lanes((8, EARLY))
    plane = fifth(e >> 6)
    r = e - 320 * plane
    in_tail = r >= 256
    slot = jnp.where(in_tail, (r - 256) >> 3, (r & 127) >> 4)
    owner = plane * 8 + (slot & 1) * 4 + (slot >> 1)
    kpos[:, 0:EARLY] = owner * HALF + jnp.where(in_tail, 32 + (r & 7), (r >> 7) * 16 + (r & 15))
    kpos[:, EARLY:] = (127 - owner) * HALF + jnp.where(
        in_tail, r & 7, 8 + (r >> 7) * 16 + (r & 15)
    )
    row = lax.broadcasted_iota(jnp.int32, (ROWS, 128), 0)
    row = row - HALF * fifth(row >> 3)
    qpos[0:ROWS] = early_pos + row
    qpos[ROWS:] = late_pos + row

    loads[0].wait()
    loads[1].wait()
    partial = jnp.dot(hidden[...], down[...], preferred_element_type=F32)
    part[0] = partial[0:48, 0:LAT]
    part[1, 0:32] = partial[48:80, 0:LAT]
    rope = jnp.concatenate([partial[:, LAT:], jnp.zeros((TOK, 128 - ROPE), F32)], 1)
    for m in range(3):
        tile = rope[32 * m : 32 * m + 16]
        if m < 2:
            tile = tile + pltpu.roll(rope[32 * m + 16 : 32 * m + 32], ROPE, 1)
        part[1, 32:48, 128 * m : 128 * m + 128] = tile
    part[1, 32:48, 384:512] = jnp.zeros((16, 128), F32)

    meet()
    cm.send("r1", part.at[1 - c], device(x, y, z, 1 - c), got1)
    cm.recv("r1", got1)
    mine[...] = part[c] + got1[...]
    cm.send("r2", mine, (seq, (1 - x_lo) * 2 + c), got2)
    cm.recv("r2", got2)
    full = mine[...] + got2[...]

    mean_square = jnp.sum(full * full, axis=1, keepdims=True) * (1.0 / LAT)
    normed = full * lax.rsqrt(mean_square + 1e-06) * gain_ref[...].astype(F32)
    cos_tiles, sin_tiles = [], []
    left = lanes((16, 128)) < 64
    for table, tiles in ((cos, cos_tiles), (sin, sin_tiles)):
        for m in range(2):
            tiles.append(
                jnp.where(left, table[32 * m : 32 * m + 16], table[32 * m + 16 : 32 * m + 32])
            )
        tiles += [table[64:80], jnp.zeros((16, 128), F32)]
    turned = rotated(
        full[32:48], jnp.concatenate(cos_tiles, 1), jnp.concatenate(sin_tiles, 1)
    )
    tail = jnp.where(c == 1, turned, normed[32:48])
    unit = jnp.concatenate([normed[0:32], tail], 0)
    unit = jnp.where(x_lo == 0, unit[:, 0:256], unit[:, 256:512]).astype(BF16)
    for g in range(2):
        KA[c, y, x, z, g] = unit[0:16, 128 * g : 128 * g + 128]
        KB[c, x, y, z, g] = unit[16:32, 128 * g : 128 * g + 128]
        KC[c, z, x, y, g] = unit[32:48, 128 * g : 128 * g + 128]
    gather_first(cm, KA, KB, KC)

    loads[2].wait()
    loads[3].wait()
    low = lanes((TOK, 128)) < 64
    for pair in range(HEADS // 2):
        t0, t1, t2 = (
            queries[:, 384 * pair + 128 * i : 384 * pair + 128 * i + 128] for i in range(3)
        )
        t1, t2 = t1.astype(F32), t2.astype(F32)
        second = pltpu.roll(jnp.where(low, t2, t1), 64, 1).astype(BF16)
        ropes = rotated(jnp.where(low, t1, t2), cos[...], sin[...]) * SCALE
        heads = []
        for i, nope in enumerate((t0, second)):
            head = 2 * pair + i
            lat = lax.dot_general(
                nope, wkey[:, 128 * head : 128 * head + 128], NT, preferred_element_type=F32
            )
            turned_q = jnp.where(low, pltpu.roll(ropes, 64, 1) if i else ropes, 0.0)
            heads.append(jnp.concatenate([lat * SCALE, turned_q], 1))
        for half in range(2):
            lo = half * HALF
            q[half * ROWS + TOK * pair : half * ROWS + TOK * pair + TOK] = jnp.concatenate(
                [heads[0][lo : lo + HALF], heads[1][lo : lo + HALF]], 0
            ).astype(BF16)
    top[...] = jnp.full_like(top, -1e30)
    total[...] = jnp.zeros_like(total)
    acc[...] = jnp.zeros_like(acc)

    gather_rest(cm, KA, KB, KC)

    def arrange(zz, carry):
        row0 = pl.multiple_of(zz * 320, 64)

        def put(row, cols, value):
            keys[pl.ds(pl.multiple_of(row, 16), value.shape[0]), cols] = value

        for yy in range(4):
            for xh in range(2):
                slot = yy * 2 + xh
                for g in range(4):
                    xx = 2 * xh + g // 2
                    cols = slice(128 * g, 128 * g + 128)
                    for core, base in ((0, 0), (1, EARLY)):
                        put(base + row0 + 16 * slot, cols, KA[core, yy, xx, zz, g % 2])
                        put(base + row0 + 128 + 16 * slot, cols, KB[core, xx, yy, zz, g % 2])
                cols = slice(512, 640)
                packed = [KC[1, zz, 2 * xh, yy, 0], KC[1, zz, 2 * xh, yy, 1]]
                swapped = [pltpu.roll(t.astype(F32), 64, 1).astype(BF16) for t in packed]
                put(row0 + 16 * slot, cols, packed[0])
                put(row0 + 128 + 16 * slot, cols, swapped[0])
                put(EARLY + row0 + 16 * slot, cols, swapped[1])
                put(EARLY + row0 + 128 + 16 * slot, cols, KC[1, zz, 2 * xh + 1, yy, 0])
        for yy in range(4):
            for g in range(5):
                cols = slice(128 * g, 128 * g + 128)
                if g < 4:
                    tiles = [KC[0, zz, 2 * xh + g // 2, yy, g % 2] for xh in range(2)]
                else:
                    tiles = [KC[1, zz, 2 * xh, yy, 1] for xh in range(2)]
                tiles = [t.astype(F32) for t in tiles]
                for base, lo in ((0, 0), (EARLY, 8)):
                    both = jnp.concatenate([t[lo : lo + 8] for t in tiles], 0).astype(BF16)
                    put(base + row0 + 256 + 16 * yy, cols, both)
        return carry

    lax.fori_loop(0, 8, arrange, 0)

    n_early = lax.div((z + 1) * 320 + STEP - 1, STEP)
    first_late = lax.div(z * 320, STEP)

    def offsets(i):
        j = i - 5
        late = 5 + jnp.minimum(first_late + j - n_early, 4)
        block = jnp.where(i < 5, i, jnp.where(j < n_early, j, late))
        rows = jnp.where((i < 5) | (j >= n_early), ROWS, 0)
        return pl.multiple_of(block * STEP, STEP), pl.multiple_of(rows, ROWS), j - n_early + first_late > 4

    def score(i, buffer):
        k0, q0, extra = offsets(i)
        s = lax.dot_general(
            q[pl.ds(q0, ROWS)], keys[pl.ds(k0, STEP)], NT, preferred_element_type=F32
        )
        limit = jnp.where(extra, -1, qpos[pl.ds(q0, ROWS)])
        allowed = kpos[0:1, pl.ds(k0, STEP)] <= jnp.concatenate([limit] * (STEP // 128), 1)
        scores[buffer] = jnp.where(allowed, s, -1e30)

    def absorb(i, buffer):
        k0, q0, _ = offsets(i)
        rows = pl.ds(q0, ROWS)
        s = scores[buffer]
        old = top[rows, 0:1]
        new = jnp.maximum(old, jnp.max(s, axis=1, keepdims=True))
        weights = jnp.exp(s - new)
        fade = jnp.exp(old - new)
        top[rows, 0:1] = new
        total[rows, 0:1] = total[rows, 0:1] * fade + jnp.sum(weights, axis=1, keepdims=True)
        product = jnp.dot(
            weights.astype(BF16), keys[pl.ds(k0, STEP), 0:LAT], preferred_element_type=F32
        )
        acc[rows] = acc[rows] * fade + product

    score(0, 0)

    def steps(n, carry):
        score(2 * n + 1, 1)
        absorb(2 * n, 0)
        score(jnp.minimum(2 * n + 2, 11), 0)
        absorb(2 * n + 1, 1)
        return carry

    lax.fori_loop(0, 6, steps, 0)

    loads[4].wait()
    for head in range(HEADS):
        halves = []
        for half in range(2):
            rows = slice(half * ROWS + head * HALF, half * ROWS + head * HALF + HALF)
            halves.append(acc[rows] / total[rows, 0:1])
        attended = jnp.concatenate(halves, 0).astype(BF16)
        cols = slice(128 * head, 128 * head + 128)
        out_ref[:, cols] = jnp.dot(
            attended, wvalue[:, cols], preferred_element_type=F32
        ).astype(BF16)
    cm.drain()


def on_device(hidden_in, w_down, kv_gain, queries, w_key, w_value):
    inverse = 10000.0 ** (-(np.arange(128) % 32) / 32.0)
    inverse = jnp.asarray(inverse.astype(np.float32)[None])
    vmem = pl.BlockSpec(memory_space=pltpu.VMEM)
    hbm = pl.BlockSpec(memory_space=pl.ANY)
    V = pltpu.VMEM
    return pl.pallas_call(
        body,
        out_shape=jax.ShapeDtypeStruct((TOK, HEADS * VDIM), BF16),
        in_specs=[hbm, hbm, vmem, vmem, hbm, hbm, hbm],
        out_specs=vmem,
        scratch_shapes=[
            V(hidden_in.shape, BF16),
            V(w_down.shape, BF16),
            V(queries.shape, BF16),
            V(w_key.shape, BF16),
            V(w_value.shape, BF16),
            V((2, 48, LAT), F32),
            V((48, LAT), F32),
            V((48, LAT), F32),
            V((48, LAT), F32),
            V((2, 4, 4, 8, 2, 16, 128), BF16),
            V((2, 4, 4, 8, 2, 16, 128), BF16),
            V((2, 8, 4, 4, 2, 16, 128), BF16),
            V((2 * EARLY, 640), BF16),
            V((2 * ROWS, 640), BF16),
            V((8, 2 * EARLY), jnp.int32),
            V((2 * ROWS, 128), jnp.int32),
            V((TOK, 128), F32),
            V((TOK, 128), F32),
            V((2, ROWS, STEP), F32),
            V((2 * ROWS, 128), F32),
            V((2 * ROWS, 128), F32),
            V((2 * ROWS, LAT), F32),
            pltpu.SemaphoreType.DMA((5,)),
            pltpu.SemaphoreType.DMA((N_SEMS,)),
            pltpu.SemaphoreType.DMA((N_SEMS,)),
        ],
        compiler_params=pltpu.CompilerParams(
            collective_id=0, has_side_effects=True, vmem_limit_bytes=56 * 2**20
        ),
        name="latent_attention",
    )(hidden_in, w_down, kv_gain.reshape(1, LAT), inverse, queries, w_key, w_value)


def solution(mesh):
    in_specs = (
        P("seq", "head"),
        P("head", None),
        P(),
        P("seq", "head"),
        P(None, "head"),
        P(None, "head"),
    )
    return jax.shard_map(
        on_device, mesh=mesh, in_specs=in_specs, out_specs=P("seq", "head"), check_vma=False
    )
```

```python
import functools

import jax
import jax.numpy as jnp
import numpy as np
from jax import lax
from jax.experimental import pallas as pl
from jax.experimental.pallas import tpu as pltpu
from jax.sharding import PartitionSpec as P

F32 = jnp.float32
BF16 = jnp.bfloat16
MESH = pl.DeviceIdType.MESH
LAT, ROPE, NOPE, VDIM = 512, 64, 128, 128
TOK, HALF, HEADS = 80, 40, 16
ROWS = HALF * HEADS
EARLY = 2560
STEP = 512
NT = (((1,), (1,)), ((), ()))
SCALE = (NOPE + ROPE) ** (-0.5)
N_SEMS = 160


def wrap(value, size):
    return lax.rem(value + 2 * size, size)


def place():
    s = lax.axis_index("seq")
    h = lax.axis_index("head")
    x = lax.rem(lax.div(s, 4), 2) * 2 + lax.div(h, 2)
    return x, lax.rem(s, 4), lax.div(s, 8), lax.rem(h, 2)


def device(x, y, z, c):
    x, y, z = wrap(x, 4), wrap(y, 4), wrap(z, 8)
    return (z * 8 + lax.div(x, 2) * 4 + y, lax.rem(x, 2) * 2 + c)


class Comm:
    def __init__(self, send_sems, recv_sems):
        self.send_sems, self.recv_sems = send_sems, recv_sems
        self.sent, self.names = [], {}

    def copy(self, name, src, dst, to):
        i = self.names.setdefault(name, len(self.names))
        return pltpu.make_async_remote_copy(
            src, dst, self.send_sems.at[i], self.recv_sems.at[i], device_id=to, device_id_type=MESH
        )

    def send(self, name, src, to, dst=None):
        copy = self.copy(name, src, src if dst is None else dst, to)
        copy.start()
        self.sent.append(copy)

    def recv(self, name, ref):
        self.copy(name, ref, ref, device(*place())).wait_recv()

    def drain(self):
        for copy in self.sent:
            copy.wait_send()
        self.sent = []


PLANE = [(dx, dy) for dx in range(4) for dy in range(4) if dx or dy]


def greet():
    x, y, z, c = place()
    bar = pltpu.get_barrier_semaphore()
    for dz in range(1, 8):
        pl.semaphore_signal(bar, 1, device_id=device(x, y, z + dz, c), device_id_type=MESH)
    for dx, dy in PLANE:
        pl.semaphore_signal(bar, 1, device_id=device(x + dx, y + dy, z, c), device_id_type=MESH)
    pl.semaphore_signal(bar, 1, device_id=device(x, y, z, 1 - c), device_id_type=MESH)


def meet():
    pl.semaphore_wait(pltpu.get_barrier_semaphore(), 7 + len(PLANE) + 1)


def gather_first(cm, kind, ref):
    x, y, z, c = place()
    if kind == "c":
        order = sorted(PLANE, key=lambda t: -(min(t[0], 4 - t[0]) + min(t[1], 4 - t[1])))
        for dx, dy in order:
            cm.send(f"cp{dx}{dy}", ref.at[c, z, x, y], device(x + dx, y + dy, z, c))
        return
    unit = ref.at[c, y, x, z] if kind == "a" else ref.at[c, x, y, z]
    for dz in (4, 3, 5, 2, 6, 1, 7):
        cm.send(f"{kind}z{dz}", unit, device(x, y, z + dz, c))


def gather_rest(cm, KA, KB, KC, arrange_a, arrange_b, arrange_c):
    x, y, z, c = place()
    sibling = device(x, y, z, 1 - c)
    other = 1 - c

    def X(d):
        return wrap(x + d, 4)

    def Y(d):
        return wrap(y + d, 4)

    def Z(d):
        return wrap(z + d, 8)

    def share(name, ref):
        cm.send("s" + name, ref, sibling)

    def col(kind, core, line, slot):
        if kind == "a":
            return KA.at[core, Y(line), X(slot)]
        return KB.at[core, X(line), Y(slot)]

    def across(kind, d):
        return device(x + d, y, z, c) if kind == "a" else device(x, y + d, z, c)

    def along(kind, d):
        return device(x, y + d, z, c) if kind == "a" else device(x + d, y, z, c)

    def start(kind):
        for dz in range(1, 8):
            unit = KA.at[c, y, x, Z(-dz)] if kind == "a" else KB.at[c, x, y, Z(-dz)]
            cm.recv(f"{kind}z{dz}", unit)
        own = col(kind, c, 0, 0)
        for d in (1, -1):
            cm.send(f"{kind}m{d}", own, across(kind, d))
        cm.send(f"{kind}m2", own, across(kind, 2))
        for d in (1, -1):
            cm.send(f"{kind}l{d}_0", own, along(kind, d))
        share(f"{kind}0_0", own)

    def middle(kind, d):
        cm.recv(f"{kind}m{d}", col(kind, c, 0, -d if d < 2 else 2))
        slot = -d if d < 2 else 2
        for e in (1, -1):
            cm.send(f"{kind}l{e}_{slot}", col(kind, c, 0, slot), along(kind, e))
        share(f"{kind}0_{slot}", col(kind, c, 0, slot))

    def last(kind, e, slot):
        cm.recv(f"{kind}l{e}_{slot}", col(kind, c, -e, slot))
        if (e == 1) == (slot in (0, 1)):
            cm.send(f"{kind}f_{slot}", col(kind, c, -e, slot), along(kind, e))
        share(f"{kind}{-e}_{slot}", col(kind, c, -e, slot))

    def far(kind, slot):
        cm.recv(f"{kind}f_{slot}", col(kind, c, 2, slot))
        share(f"{kind}2_{slot}", col(kind, c, 2, slot))

    def ring(k, part):
        rows = slice(2 * part, 2 * part + 2)
        for d in (1, -1):
            block = KC.at[c, Z(-d * k), rows]
            if k > 0:
                cm.recv(f"cz{d}_{k}_{part}", block)
            if k < 3 or (d == 1) == (part == 0):
                cm.send(f"cz{d}_{k + 1}_{part}", block, device(x, y, z + d, c))
            if k > 0:
                share(f"c{d * k}_{part}", block)

    for dx, dy in PLANE:
        cm.recv(f"cp{dx}{dy}", KC.at[c, z, X(-dx), Y(-dy)])
    ring(0, 0)
    ring(0, 1)
    share("c0", KC.at[c, z])
    start("a")
    start("b")
    ring(1, 0)
    ring(1, 1)
    for d in (1, -1):
        middle("a", d)
        middle("b", d)
    ring(2, 0)
    last("a", 1, 0)
    last("b", 1, 0)
    middle("a", 2)
    middle("b", 2)
    ring(2, 1)
    for e, slot in ((1, 1), (-1, -1)):
        last("a", e, slot)
        last("b", e, slot)
    ring(3, 0)
    for e, slot in ((-1, 2), (-1, 0)):
        last("a", e, slot)
        last("b", e, slot)
    ring(3, 1)
    for e, slot in ((1, -1), (-1, 1), (1, 2)):
        last("a", e, slot)
        last("b", e, slot)

    def line_from_sibling(kind, d):
        for slot in (0, 1, -1, 2):
            cm.recv(f"s{kind}{d}_{slot}", col(kind, other, d, slot))

    def planes_from_sibling(k):
        for part in range(2):
            cm.recv(f"sc{k}_{part}", KC.at[other, Z(-k), 2 * part : 2 * part + 2])

    line_from_sibling("a", 0)
    arrange_a(Y(0))
    cm.recv("sc0", KC.at[other, z])
    arrange_c(z)
    for k in (1, -1, 2, -2):
        planes_from_sibling(k)
    lax.fori_loop(0, 4, lambda i, carry: (arrange_c(Z(jnp.where(i < 2, i - 2, i - 1))), carry)[1], 0)
    for d in (1, -1):
        line_from_sibling("a", d)
        arrange_a(Y(d))
    for part in range(2):
        block = KC.at[c, Z(4), 2 * part : 2 * part + 2]
        cm.recv(f"cz{1 if part == 0 else -1}_4_{part}", block)
        share(f"c4_{part}", block)
    for slot in (0, 1, -1, 2):
        far("a", slot)
        far("b", slot)
    for d in (0, 1, -1):
        line_from_sibling("b", d)
    arrange_b(x >> 1)
    for k in (3, -3, 4):
        planes_from_sibling(k)
    lax.fori_loop(0, 3, lambda i, carry: (arrange_c(Z(i + 3)), carry)[1], 0)
    line_from_sibling("a", 2)
    arrange_a(Y(2))
    line_from_sibling("b", 2)
    arrange_b(1 - (x >> 1))


def lanes(shape):
    return lax.broadcasted_iota(jnp.int32, shape, 1)


def rotated(v, cos, sin):
    width = v.shape[1]
    first = (lanes(v.shape) & 63) < 32
    other = jnp.where(first, pltpu.roll(v, width - 32, 1), pltpu.roll(v, 32, 1))
    return v * cos + other * sin


def fifth(value):
    return (value * 205) >> 10


def body(
    hidden_hbm, down_hbm, gain_ref, inv_ref, queries_hbm, wkey_hbm, wvalue_hbm, out_ref,
    hidden, down, queries, wkey, wvalue, part, got1, mine, got2, KA, KB, KC,
    keys, q, kpos, qpos, cos, sin, scores, top, total, acc,
    load_sems, send_sems, recv_sems,
):
    x, y, z, c = place()
    seq = lax.axis_index("seq")
    x_lo = lax.rem(x, 2)
    loads = [
        pltpu.make_async_copy(src, dst, load_sems.at[i])
        for i, (src, dst) in enumerate(
            (
                (hidden_hbm, hidden),
                (down_hbm, down),
                (queries_hbm, queries),
                (wkey_hbm, wkey),
                (wvalue_hbm, wvalue),
            )
        )
    ]
    for load in loads[:2]:
        load.start()
    greet()
    cm = Comm(send_sems, recv_sems)

    token = lax.broadcasted_iota(jnp.int32, (TOK, 128), 0)
    lane = lanes((TOK, 128))
    early_pos = seq * HALF
    late_pos = (127 - seq) * HALF
    position = jnp.where(token < HALF, early_pos + token, late_pos + token - HALF)
    angle = position.astype(F32) * inv_ref[...]
    cos[...] = jnp.cos(angle)
    sine = jnp.sin(angle)
    sin[...] = jnp.where((lane & 63) < 32, -sine, sine)

    e = lanes((8, EARLY))
    plane = fifth(e >> 6)
    r = e - 320 * plane
    in_tail = r >= 256
    slot = jnp.where(in_tail, (r - 256) >> 3, (r & 127) >> 4)
    owner = plane * 8 + (slot & 1) * 4 + (slot >> 1)
    kpos[:, 0:EARLY] = owner * HALF + jnp.where(in_tail, 32 + (r & 7), (r >> 7) * 16 + (r & 15))
    kpos[:, EARLY:] = (127 - owner) * HALF + jnp.where(
        in_tail, r & 7, 8 + (r >> 7) * 16 + (r & 15)
    )
    row = lax.broadcasted_iota(jnp.int32, (ROWS, 128), 0)
    row = row - HALF * fifth(row >> 3)
    qpos[0:ROWS] = early_pos + row
    qpos[ROWS:] = late_pos + row

    loads[0].wait()
    loads[1].wait()
    for load in loads[2:]:
        load.start()
    partial = lax.dot_general(hidden[...], down[...], NT, preferred_element_type=F32)
    part[0] = partial[0:48, 0:LAT]
    part[1, 0:32] = partial[48:80, 0:LAT]
    rope = jnp.concatenate([partial[:, LAT:], jnp.zeros((TOK, 128 - ROPE), F32)], 1)
    for m in range(3):
        tile = rope[32 * m : 32 * m + 16]
        if m < 2:
            tile = tile + pltpu.roll(rope[32 * m + 16 : 32 * m + 32], ROPE, 1)
        part[1, 32:48, 128 * m : 128 * m + 128] = tile
    part[1, 32:48, 384:512] = jnp.zeros((16, 128), F32)

    meet()
    tiles = [slice(16 * t, 16 * t + 16) for t in range(3)]
    order = (2, 0, 1)
    for t in order:
        cm.send(f"r1_{t}", part.at[1 - c, tiles[t]], device(x, y, z, 1 - c), got1.at[tiles[t]])
    for t in order:
        cm.recv(f"r1_{t}", got1.at[tiles[t]])
        mine[tiles[t]] = part[c, tiles[t]] + got1[tiles[t]]
        cm.send(
            f"r2_{t}", mine.at[tiles[t]], (seq, (1 - x_lo) * 2 + c), got2.at[tiles[t]]
        )
    gain = gain_ref[...].astype(F32).reshape(1, LAT)
    cos_tiles, sin_tiles = [], []
    left = lanes((16, 128)) < 64
    for table, picked in ((cos, cos_tiles), (sin, sin_tiles)):
        for m in range(2):
            picked.append(
                jnp.where(left, table[32 * m : 32 * m + 16], table[32 * m + 16 : 32 * m + 32])
            )
        picked += [table[64:80], jnp.zeros((16, 128), F32)]
    cos_keys, sin_keys = jnp.concatenate(cos_tiles, 1), jnp.concatenate(sin_tiles, 1)
    for t in order:
        cm.recv(f"r2_{t}", got2.at[tiles[t]])
        full = mine[tiles[t]] + got2[tiles[t]]
        mean_square = jnp.sum(full * full, axis=1, keepdims=True) * (1.0 / LAT)
        unit = full * lax.rsqrt(mean_square + 1e-06) * gain
        if t == 2:
            unit = jnp.where(c == 1, rotated(full, cos_keys, sin_keys), unit)
        unit = jnp.where(x_lo == 0, unit[:, 0:256], unit[:, 256:512]).astype(BF16)
        for g in range(2):
            tile = unit[:, 128 * g : 128 * g + 128]
            if t == 0:
                KA[c, y, x, z, g] = tile
            elif t == 1:
                KB[c, x, y, z, g] = tile
            else:
                KC[c, z, x, y, g] = tile
        gather_first(cm, "abc"[t], (KA, KB, KC)[t])

    loads[2].wait()
    loads[3].wait()
    low = lanes((TOK, 128)) < 64
    for pair in range(HEADS // 2):
        t0, t1, t2 = (
            queries[:, 384 * pair + 128 * i : 384 * pair + 128 * i + 128] for i in range(3)
        )
        t1, t2 = t1.astype(F32), t2.astype(F32)
        second = pltpu.roll(jnp.where(low, t2, t1), 64, 1).astype(BF16)
        ropes = rotated(jnp.where(low, t1, t2), cos[...], sin[...]) * SCALE
        heads = []
        for i, nope in enumerate((t0, second)):
            head = 2 * pair + i
            lat = lax.dot_general(
                nope, wkey[:, 128 * head : 128 * head + 128], NT, preferred_element_type=F32
            )
            turned_q = jnp.where(low, pltpu.roll(ropes, 64, 1) if i else ropes, 0.0)
            heads.append(jnp.concatenate([lat * SCALE, turned_q], 1))
        for half in range(2):
            lo = half * HALF
            q[half * ROWS + TOK * pair : half * ROWS + TOK * pair + TOK] = jnp.concatenate(
                [heads[0][lo : lo + HALF], heads[1][lo : lo + HALF]], 0
            ).astype(BF16)
    top[...] = jnp.full_like(top, -1e30)
    total[...] = jnp.zeros_like(total)
    acc[...] = jnp.zeros_like(acc)


    def put(row, cols, value):
        keys[pl.ds(pl.multiple_of(row, 16), value.shape[0]), cols] = value

    def arrange_a(yy):
        def one(zz, carry):
            for xh in range(2):
                for g in range(4):
                    cols = slice(128 * g, 128 * g + 128)
                    for core in range(2):
                        row = core * EARLY + zz * 320 + 16 * (yy * 2 + xh)
                        put(row, cols, KA[core, yy, 2 * xh + g // 2, zz, g % 2])
            return carry

        lax.fori_loop(0, 8, one, 0)

    def arrange_b(xh):
        def one(zz, carry):
            for yy in range(4):
                for g in range(4):
                    cols = slice(128 * g, 128 * g + 128)
                    for core in range(2):
                        row = core * EARLY + zz * 320 + 128 + 16 * (yy * 2 + xh)
                        put(row, cols, KB[core, 2 * xh + g // 2, yy, zz, g % 2])
            return carry

        lax.fori_loop(0, 8, one, 0)

    def arrange_c(zz):
        row0 = zz * 320
        for yy in range(4):
            for xh in range(2):
                slot = yy * 2 + xh
                cols = slice(512, 640)
                packed = [KC[1, zz, 2 * xh, yy, g] for g in range(2)]
                swapped = [pltpu.roll(t.astype(F32), 64, 1).astype(BF16) for t in packed]
                put(row0 + 16 * slot, cols, packed[0])
                put(row0 + 128 + 16 * slot, cols, swapped[0])
                put(EARLY + row0 + 16 * slot, cols, swapped[1])
                put(EARLY + row0 + 128 + 16 * slot, cols, KC[1, zz, 2 * xh + 1, yy, 0])
        for yy in range(4):
            for g in range(5):
                cols = slice(128 * g, 128 * g + 128)
                if g < 4:
                    both = [KC[0, zz, 2 * xh + g // 2, yy, g % 2] for xh in range(2)]
                else:
                    both = [KC[1, zz, 2 * xh, yy, 1] for xh in range(2)]
                both = [t.astype(F32) for t in both]
                for base, lo in ((0, 0), (EARLY, 8)):
                    rows = jnp.concatenate([t[lo : lo + 8] for t in both], 0).astype(BF16)
                    put(base + row0 + 256 + 16 * yy, cols, rows)

    gather_rest(cm, KA, KB, KC, arrange_a, arrange_b, arrange_c)

    n_early = lax.div((z + 1) * 320 + STEP - 1, STEP)
    first_late = lax.div(z * 320, STEP)

    def offsets(i):
        j = i - 5
        late = 5 + jnp.minimum(first_late + j - n_early, 4)
        block = jnp.where(i < 5, i, jnp.where(j < n_early, j, late))
        rows = jnp.where((i < 5) | (j >= n_early), ROWS, 0)
        return pl.multiple_of(block * STEP, STEP), pl.multiple_of(rows, ROWS), j - n_early + first_late > 4

    def score(i, buffer):
        k0, q0, extra = offsets(i)
        s = lax.dot_general(
            q[pl.ds(q0, ROWS)], keys[pl.ds(k0, STEP)], NT, preferred_element_type=F32
        )
        limit = jnp.where(extra, -1, qpos[pl.ds(q0, ROWS)])
        allowed = kpos[0:1, pl.ds(k0, STEP)] <= jnp.concatenate([limit] * (STEP // 128), 1)
        scores[buffer] = jnp.where(allowed, s, -1e30)

    def absorb(i, buffer):
        k0, q0, _ = offsets(i)
        rows = pl.ds(q0, ROWS)
        s = scores[buffer]
        old = top[rows]
        new = jnp.maximum(old, jnp.max(s, axis=1, keepdims=True))
        weights = jnp.exp(s - jnp.concatenate([new] * (STEP // 128), 1))
        fade = jnp.exp(old - new)
        top[rows] = new
        total[rows] = total[rows] * fade + (
            (weights[:, 0:128] + weights[:, 128:256]) + (weights[:, 256:384] + weights[:, 384:512])
        )
        product = jnp.dot(
            weights.astype(BF16), keys[pl.ds(k0, STEP), 0:LAT], preferred_element_type=F32
        )
        acc[rows] = acc[rows] * jnp.concatenate([fade] * (LAT // 128), 1) + product

    score(0, 0)

    def steps(n, carry):
        absorb(2 * n, 0)
        score(2 * n + 1, 1)
        absorb(2 * n + 1, 1)
        score(jnp.minimum(2 * n + 2, 11), 0)
        return carry

    lax.fori_loop(0, 6, steps, 0)

    loads[4].wait()
    for head in range(HEADS):
        halves = []
        for half in range(2):
            rows = slice(half * ROWS + head * HALF, half * ROWS + head * HALF + HALF)
            halves.append(acc[rows] / jnp.sum(total[rows], axis=1, keepdims=True))
        attended = jnp.concatenate(halves, 0).astype(BF16)
        cols = slice(128 * head, 128 * head + 128)
        out_ref[:, cols] = jnp.dot(
            attended, wvalue[:, cols], preferred_element_type=F32
        ).astype(BF16)
    cm.drain()


def on_device(hidden_in, w_down, kv_gain, queries, w_key, w_value):
    inverse = 10000.0 ** (-(np.arange(128) % 32) / 32.0)
    inverse = jnp.asarray(inverse.astype(np.float32)[None])
    vmem = pl.BlockSpec(memory_space=pltpu.VMEM)
    hbm = pl.BlockSpec(memory_space=pl.ANY)
    V = pltpu.VMEM
    return pl.pallas_call(
        body,
        out_shape=jax.ShapeDtypeStruct((TOK, HEADS * VDIM), BF16),
        in_specs=[hbm, hbm, vmem, vmem, hbm, hbm, hbm],
        out_specs=vmem,
        scratch_shapes=[
            V(hidden_in.shape, BF16),
            V(w_down.shape[::-1], BF16),
            V(queries.shape, BF16),
            V(w_key.shape, BF16),
            V(w_value.shape, BF16),
            V((2, 48, LAT), F32),
            V((48, LAT), F32),
            V((48, LAT), F32),
            V((48, LAT), F32),
            V((2, 4, 4, 8, 2, 16, 128), BF16),
            V((2, 4, 4, 8, 2, 16, 128), BF16),
            V((2, 8, 4, 4, 2, 16, 128), BF16),
            V((2 * EARLY, 640), BF16),
            V((2 * ROWS, 640), BF16),
            V((8, 2 * EARLY), jnp.int32),
            V((2 * ROWS, 128), jnp.int32),
            V((TOK, 128), F32),
            V((TOK, 128), F32),
            V((2, ROWS, STEP), F32),
            V((2 * ROWS, 128), F32),
            V((2 * ROWS, 128), F32),
            V((2 * ROWS, LAT), F32),
            pltpu.SemaphoreType.DMA((5,)),
            pltpu.SemaphoreType.DMA((N_SEMS,)),
            pltpu.SemaphoreType.DMA((N_SEMS,)),
        ],
        compiler_params=pltpu.CompilerParams(
            collective_id=0, has_side_effects=True, vmem_limit_bytes=56 * 2**20
        ),
        name="latent_attention",
    )(hidden_in, w_down.T, kv_gain, inverse, queries, w_key, w_value)


def solution(mesh):
    in_specs = (
        P("seq", "head"),
        P("head", None),
        P(),
        P("seq", "head"),
        P(None, "head"),
        P(None, "head"),
    )
    return jax.shard_map(
        on_device, mesh=mesh, in_specs=in_specs, out_specs=P("seq", "head"), check_vma=False
    )
```

```python
import functools

import jax
import jax.numpy as jnp
import numpy as np
from jax import lax
from jax.experimental import pallas as pl
from jax.experimental.pallas import tpu as pltpu
from jax.sharding import PartitionSpec as P

F32 = jnp.float32
BF16 = jnp.bfloat16
MESH = pl.DeviceIdType.MESH
LAT, ROPE, NOPE, VDIM = 512, 64, 128, 128
TOK, HALF, HEADS = 80, 40, 16
ROWS = HALF * HEADS
EARLY = 2560
STEP = 1280
DEEP = 896
NT = (((1,), (1,)), ((), ()))
SCALE = (NOPE + ROPE) ** (-0.5)
N_SEMS = 160


def wrap(value, size):
    return value & (size - 1)


def place():
    s = lax.axis_index("seq")
    h = lax.axis_index("head")
    return ((s >> 2) & 1) * 2 + (h >> 1), s & 3, s >> 3, h & 1


def device(x, y, z, c):
    x, y, z = wrap(x, 4), wrap(y, 4), wrap(z, 8)
    return (z * 8 + (x >> 1) * 4 + y, (x & 1) * 2 + c)


class Comm:
    def __init__(self, send_sems, recv_sems):
        self.send_sems, self.recv_sems = send_sems, recv_sems
        self.sent, self.names = [], {}

    def copy(self, name, src, dst, to):
        i = self.names.setdefault(name, len(self.names))
        return pltpu.make_async_remote_copy(
            src, dst, self.send_sems.at[i], self.recv_sems.at[i], device_id=to, device_id_type=MESH
        )

    def send(self, name, src, to, dst=None):
        copy = self.copy(name, src, src if dst is None else dst, to)
        copy.start()
        self.sent.append(copy)

    def recv(self, name, ref):
        self.copy(name, ref, ref, device(*place())).wait_recv()

    def drain(self):
        for copy in self.sent:
            copy.wait_send()
        self.sent = []


PLANE = [(dx, dy) for dx in range(4) for dy in range(4) if dx or dy]


def greet():
    x, y, z, c = place()
    bar = pltpu.get_barrier_semaphore()
    for dz in range(1, 8):
        pl.semaphore_signal(bar, 1, device_id=device(x, y, z + dz, c), device_id_type=MESH)
    for dx, dy in PLANE:
        pl.semaphore_signal(bar, 1, device_id=device(x + dx, y + dy, z, c), device_id_type=MESH)
    pl.semaphore_signal(bar, 1, device_id=device(x, y, z, 1 - c), device_id_type=MESH)


def meet():
    pl.semaphore_wait(pltpu.get_barrier_semaphore(), 7 + len(PLANE) + 1)


def gather_first(cm, kind, ref):
    x, y, z, c = place()
    if kind == "c":
        order = sorted(PLANE, key=lambda t: -(min(t[0], 4 - t[0]) + min(t[1], 4 - t[1])))
        for dx, dy in order:
            cm.send(f"cp{dx}{dy}", ref.at[c, z, x, y], device(x + dx, y + dy, z, c))
        return
    unit = ref.at[c, y, x, z] if kind == "a" else ref.at[c, x, y, z]
    for dz in (4, 3, 5, 2, 6, 1, 7):
        cm.send(f"{kind}z{dz}", unit, device(x, y, z + dz, c))


def gather_rest(cm, KA, KB, KC, arrange_a, arrange_b, arrange_c):
    x, y, z, c = place()
    sibling = device(x, y, z, 1 - c)
    other = 1 - c

    def X(d):
        return wrap(x + d, 4)

    def Y(d):
        return wrap(y + d, 4)

    def Z(d):
        return wrap(z + d, 8)

    def share(name, ref):
        cm.send("s" + name, ref, sibling)

    def col(kind, core, line, slot):
        if kind == "a":
            return KA.at[core, Y(line), X(slot)]
        return KB.at[core, X(line), Y(slot)]

    def across(kind, d):
        return device(x + d, y, z, c) if kind == "a" else device(x, y + d, z, c)

    def along(kind, d):
        return device(x, y + d, z, c) if kind == "a" else device(x + d, y, z, c)

    def start(kind):
        for dz in range(1, 8):
            unit = KA.at[c, y, x, Z(-dz)] if kind == "a" else KB.at[c, x, y, Z(-dz)]
            cm.recv(f"{kind}z{dz}", unit)
        own = col(kind, c, 0, 0)
        for d in (1, -1):
            cm.send(f"{kind}m{d}", own, across(kind, d))
        cm.send(f"{kind}m2", own, across(kind, 2))
        for d in (1, -1):
            cm.send(f"{kind}l{d}_0", own, along(kind, d))
        share(f"{kind}0_0", own)

    def middle(kind, d):
        cm.recv(f"{kind}m{d}", col(kind, c, 0, -d if d < 2 else 2))
        slot = -d if d < 2 else 2
        for e in (1, -1):
            cm.send(f"{kind}l{e}_{slot}", col(kind, c, 0, slot), along(kind, e))
        share(f"{kind}0_{slot}", col(kind, c, 0, slot))

    def last(kind, e, slot):
        cm.recv(f"{kind}l{e}_{slot}", col(kind, c, -e, slot))
        if (e == 1) == (slot in (0, 1)):
            cm.send(f"{kind}f_{slot}", col(kind, c, -e, slot), along(kind, e))
        share(f"{kind}{-e}_{slot}", col(kind, c, -e, slot))

    def far(kind, slot):
        cm.recv(f"{kind}f_{slot}", col(kind, c, 2, slot))
        share(f"{kind}2_{slot}", col(kind, c, 2, slot))

    def ring(k, part):
        rows = slice(2 * part, 2 * part + 2)
        for d in (1, -1):
            block = KC.at[c, Z(-d * k), rows]
            if k > 0:
                cm.recv(f"cz{d}_{k}_{part}", block)
            if k < 3 or (d == 1) == (part == 0):
                cm.send(f"cz{d}_{k + 1}_{part}", block, device(x, y, z + d, c))
            if k > 0:
                share(f"c{d * k}_{part}", block)

    for dx, dy in PLANE:
        cm.recv(f"cp{dx}{dy}", KC.at[c, z, X(-dx), Y(-dy)])
    ring(0, 0)
    ring(0, 1)
    share("c0", KC.at[c, z])
    start("a")
    start("b")
    ring(1, 0)
    ring(1, 1)
    for kind in "ab":
        middle(kind, 1)
    for kind in "ab":
        middle(kind, -1)
    ring(2, 0)
    ring(2, 1)
    for kind in "ab":
        last(kind, 1, 0)
    for kind in "ab":
        middle(kind, 2)
    for kind in "ab":
        last(kind, 1, 1)
    for kind in "ab":
        last(kind, -1, -1)
    ring(3, 0)
    ring(3, 1)
    for kind in "ab":
        last(kind, -1, 2)
    for kind in "ab":
        last(kind, -1, 0)
    for kind in "ab":
        last(kind, 1, -1)
    for kind in "ab":
        last(kind, -1, 1)
    for kind in "ab":
        last(kind, 1, 2)

    def line_from_sibling(kind, d):
        for slot in (0, 1, -1, 2):
            cm.recv(f"s{kind}{d}_{slot}", col(kind, other, d, slot))

    def planes_from_sibling(k):
        for part in range(2):
            cm.recv(f"sc{k}_{part}", KC.at[other, Z(-k), 2 * part : 2 * part + 2])

    line_from_sibling("a", 0)
    arrange_a(Y(0))
    cm.recv("sc0", KC.at[other, z])
    arrange_c(z)
    for k in (1, -1, 2, -2):
        planes_from_sibling(k)
    lax.fori_loop(0, 4, lambda i, carry: (arrange_c(Z(jnp.where(i < 2, i - 2, i - 1))), carry)[1], 0)
    for d in (1, -1):
        line_from_sibling("a", d)
        arrange_a(Y(d))
    for part in range(2):
        block = KC.at[c, Z(4), 2 * part : 2 * part + 2]
        cm.recv(f"cz{1 if part == 0 else -1}_4_{part}", block)
        share(f"c4_{part}", block)
    for slot in (0, 1, -1, 2):
        far("a", slot)
        far("b", slot)
    for d in (0, 1, -1):
        line_from_sibling("b", d)
    arrange_b(x >> 1)
    for k in (3, -3, 4):
        planes_from_sibling(k)
    lax.fori_loop(0, 3, lambda i, carry: (arrange_c(Z(i + 3)), carry)[1], 0)
    line_from_sibling("a", 2)
    arrange_a(Y(2))
    line_from_sibling("b", 2)
    arrange_b(1 - (x >> 1))


def lanes(shape):
    return lax.broadcasted_iota(jnp.int32, shape, 1)


def rotated(v, cos, sin):
    width = v.shape[1]
    first = (lanes(v.shape) & 63) < 32
    other = jnp.where(first, pltpu.roll(v, width - 32, 1), pltpu.roll(v, 32, 1))
    return v * cos + other * sin


def fifth(value):
    return (value * 205) >> 10


def body(
    hidden_hbm, down_hbm, gain_ref, inv_ref, queries_hbm, wkey_hbm, wvalue_hbm, out_hbm,
    hidden, down, queries, wkey, wvalue, result, part, got1, mine, got2, KA, KB, KC,
    keys, q, kpos, qpos, cos, sin, scores, top, total, acc,
    load_sems, send_sems, recv_sems,
):
    x, y, z, c = place()
    seq = lax.axis_index("seq")
    x_lo = x & 1
    loads = [
        pltpu.make_async_copy(src, dst, load_sems.at[i])
        for i, (src, dst) in enumerate(
            (
                (hidden_hbm, hidden),
                (down_hbm.at[:, 0:DEEP], down.at[:, 0:DEEP]),
                (down_hbm.at[:, DEEP:], down.at[:, DEEP:]),
                (queries_hbm, queries),
                (wkey_hbm, wkey),
                (wvalue_hbm, wvalue),
            )
        )
    ]
    for load in loads[:3]:
        load.start()
    greet()
    cm = Comm(send_sems, recv_sems)

    token = lax.broadcasted_iota(jnp.int32, (TOK, 128), 0)
    lane = lanes((TOK, 128))
    early_pos = seq * HALF
    late_pos = (127 - seq) * HALF
    position = jnp.where(token < HALF, early_pos + token, late_pos + token - HALF)
    angle = position.astype(F32) * inv_ref[...]
    cos[...] = jnp.cos(angle)
    sine = jnp.sin(angle)
    sin[...] = jnp.where((lane & 63) < 32, -sine, sine)

    e = lanes((8, EARLY))
    plane = fifth(e >> 6)
    r = e - 320 * plane
    in_tail = r >= 256
    slot = jnp.where(in_tail, (r - 256) >> 3, (r & 127) >> 4)
    owner = plane * 8 + (slot & 1) * 4 + (slot >> 1)
    kpos[:, 0:EARLY] = owner * HALF + jnp.where(in_tail, 32 + (r & 7), (r >> 7) * 16 + (r & 15))
    kpos[:, EARLY:] = (127 - owner) * HALF + jnp.where(
        in_tail, r & 7, 8 + (r >> 7) * 16 + (r & 15)
    )
    row = lax.broadcasted_iota(jnp.int32, (ROWS, 128), 0)
    row = row - HALF * fifth(row >> 3)
    qpos[0:ROWS] = early_pos + row
    qpos[ROWS:] = late_pos + row

    loads[0].wait()
    loads[1].wait()
    for load in loads[3:]:
        load.start()
    partial = lax.dot_general(
        hidden[:, 0:DEEP], down[:, 0:DEEP], NT, preferred_element_type=F32
    )
    loads[2].wait()
    partial = partial + lax.dot_general(
        hidden[:, DEEP:], down[:, DEEP:], NT, preferred_element_type=F32
    )
    part[0] = partial[0:48, 0:LAT]
    part[1, 0:32] = partial[48:80, 0:LAT]
    rope = jnp.concatenate([partial[:, LAT:], jnp.zeros((TOK, 128 - ROPE), F32)], 1)
    for m in range(3):
        tile = rope[32 * m : 32 * m + 16]
        if m < 2:
            tile = tile + pltpu.roll(rope[32 * m + 16 : 32 * m + 32], ROPE, 1)
        part[1, 32:48, 128 * m : 128 * m + 128] = tile
    part[1, 32:48, 384:512] = jnp.zeros((16, 128), F32)

    meet()
    tiles = [slice(16 * t, 16 * t + 16) for t in range(3)]
    order = (2, 0, 1)
    for t in order:
        cm.send(f"r1_{t}", part.at[1 - c, tiles[t]], device(x, y, z, 1 - c), got1.at[tiles[t]])
    for t in order:
        cm.recv(f"r1_{t}", got1.at[tiles[t]])
        mine[tiles[t]] = part[c, tiles[t]] + got1[tiles[t]]
        cm.send(
            f"r2_{t}", mine.at[tiles[t]], (seq, (1 - x_lo) * 2 + c), got2.at[tiles[t]]
        )
    gain = gain_ref[...].astype(F32).reshape(1, LAT)
    cos_tiles, sin_tiles = [], []
    left = lanes((16, 128)) < 64
    for table, picked in ((cos, cos_tiles), (sin, sin_tiles)):
        for m in range(2):
            picked.append(
                jnp.where(left, table[32 * m : 32 * m + 16], table[32 * m + 16 : 32 * m + 32])
            )
        picked += [table[64:80], jnp.zeros((16, 128), F32)]
    cos_keys, sin_keys = jnp.concatenate(cos_tiles, 1), jnp.concatenate(sin_tiles, 1)
    for t in order:
        cm.recv(f"r2_{t}", got2.at[tiles[t]])
        full = mine[tiles[t]] + got2[tiles[t]]
        mean_square = jnp.sum(full * full, axis=1, keepdims=True) * (1.0 / LAT)
        unit = full * lax.rsqrt(mean_square + 1e-06) * gain
        if t == 2:
            unit = jnp.where(c == 1, rotated(full, cos_keys, sin_keys), unit)
        unit = jnp.where(x_lo == 0, unit[:, 0:256], unit[:, 256:512]).astype(BF16)
        for g in range(2):
            tile = unit[:, 128 * g : 128 * g + 128]
            if t == 0:
                KA[c, y, x, z, g] = tile
            elif t == 1:
                KB[c, x, y, z, g] = tile
            else:
                KC[c, z, x, y, g] = tile
        gather_first(cm, "abc"[t], (KA, KB, KC)[t])

    loads[3].wait()
    loads[4].wait()
    low = lanes((TOK, 128)) < 64
    for pair in range(HEADS // 2):
        t0, t1, t2 = (
            queries[:, 384 * pair + 128 * i : 384 * pair + 128 * i + 128] for i in range(3)
        )
        t1, t2 = t1.astype(F32), t2.astype(F32)
        second = pltpu.roll(jnp.where(low, t2, t1), 64, 1).astype(BF16)
        ropes = rotated(jnp.where(low, t1, t2), cos[...], sin[...]) * SCALE
        heads = []
        for i, nope in enumerate((t0, second)):
            head = 2 * pair + i
            lat = lax.dot_general(
                nope, wkey[:, 128 * head : 128 * head + 128], NT, preferred_element_type=F32
            )
            turned_q = jnp.where(low, pltpu.roll(ropes, 64, 1) if i else ropes, 0.0)
            heads.append(jnp.concatenate([lat * SCALE, turned_q], 1))
        for half in range(2):
            lo = half * HALF
            q[half * ROWS + TOK * pair : half * ROWS + TOK * pair + TOK] = jnp.concatenate(
                [heads[0][lo : lo + HALF], heads[1][lo : lo + HALF]], 0
            ).astype(BF16)
    top[...] = jnp.full_like(top, -1e30)
    total[...] = jnp.zeros_like(total)
    acc[...] = jnp.zeros_like(acc)


    def put(row, cols, value):
        keys[pl.ds(pl.multiple_of(row, 16), value.shape[0]), cols] = value

    def arrange_a(yy):
        def one(zz, carry):
            for xh in range(2):
                for g in range(4):
                    cols = slice(128 * g, 128 * g + 128)
                    for core in range(2):
                        row = core * EARLY + zz * 320 + 16 * (yy * 2 + xh)
                        put(row, cols, KA[core, yy, 2 * xh + g // 2, zz, g % 2])
            return carry

        lax.fori_loop(0, 8, one, 0)

    def arrange_b(xh):
        def one(zz, carry):
            for yy in range(4):
                for g in range(4):
                    cols = slice(128 * g, 128 * g + 128)
                    for core in range(2):
                        row = core * EARLY + zz * 320 + 128 + 16 * (yy * 2 + xh)
                        put(row, cols, KB[core, 2 * xh + g // 2, yy, zz, g % 2])
            return carry

        lax.fori_loop(0, 8, one, 0)

    def arrange_c(zz):
        row0 = zz * 320
        for yy in range(4):
            for xh in range(2):
                slot = yy * 2 + xh
                cols = slice(512, 640)
                packed = [KC[1, zz, 2 * xh, yy, g] for g in range(2)]
                swapped = [pltpu.roll(t.astype(F32), 64, 1).astype(BF16) for t in packed]
                put(row0 + 16 * slot, cols, packed[0])
                put(row0 + 128 + 16 * slot, cols, swapped[0])
                put(EARLY + row0 + 16 * slot, cols, swapped[1])
                put(EARLY + row0 + 128 + 16 * slot, cols, KC[1, zz, 2 * xh + 1, yy, 0])
        for yy in range(4):
            for g in range(5):
                cols = slice(128 * g, 128 * g + 128)
                if g < 4:
                    both = [KC[0, zz, 2 * xh + g // 2, yy, g % 2] for xh in range(2)]
                else:
                    both = [KC[1, zz, 2 * xh, yy, 1] for xh in range(2)]
                both = [t.astype(F32) for t in both]
                for base, lo in ((0, 0), (EARLY, 8)):
                    rows = jnp.concatenate([t[lo : lo + 8] for t in both], 0).astype(BF16)
                    put(base + row0 + 256 + 16 * yy, cols, rows)

    gather_rest(cm, KA, KB, KC, arrange_a, arrange_b, arrange_c)

    upper = z >= 4

    def offsets(i):
        fourth = jnp.where(upper, 1, 2)
        block = jnp.where(i < 2, i, jnp.where(i == 2, 0, jnp.where(i == 3, fourth, 3)))
        rows = jnp.where((i == 2) | ((i == 3) & upper), 0, ROWS)
        return pl.multiple_of(block * STEP, STEP), pl.multiple_of(rows, ROWS)

    def score(i, buffer):
        k0, q0 = offsets(i)
        s = lax.dot_general(
            q[pl.ds(q0, ROWS)], keys[pl.ds(k0, STEP)], NT, preferred_element_type=F32
        )
        limit = qpos[pl.ds(q0, ROWS)]
        allowed = kpos[0:1, pl.ds(k0, STEP)] <= jnp.concatenate([limit] * (STEP // 128), 1)
        scores[buffer] = jnp.where(allowed, s, -1e30)

    def absorb(i, buffer):
        k0, q0 = offsets(i)
        rows = pl.ds(q0, ROWS)
        s = scores[buffer]
        old = top[rows]
        new = jnp.maximum(old, jnp.max(s, axis=1, keepdims=True))
        weights = jnp.exp(s - jnp.concatenate([new] * (STEP // 128), 1))
        fade = jnp.exp(old - new)
        top[rows] = new
        total[rows] = total[rows] * fade + (
            sum(weights[:, i : i + 128] for i in range(0, STEP, 128))
        )
        product = jnp.dot(
            weights.astype(BF16), keys[pl.ds(k0, STEP), 0:LAT], preferred_element_type=F32
        )
        acc[rows] = acc[rows] * jnp.concatenate([fade] * (LAT // 128), 1) + product

    score(0, 0)

    def steps(n, carry):
        absorb(2 * n, 0)
        score(2 * n + 1, 1)
        absorb(2 * n + 1, 1)
        score(2 * n + 2, 0)
        return carry

    lax.fori_loop(0, 2, steps, 0)
    absorb(4, 0)

    loads[5].wait()
    leaving = []
    for head in range(HEADS):
        halves = []
        for half in range(2):
            rows = slice(half * ROWS + head * HALF, half * ROWS + head * HALF + HALF)
            halves.append(acc[rows] * (1.0 / jnp.sum(total[rows], axis=1, keepdims=True)))
        attended = jnp.concatenate(halves, 0).astype(BF16)
        cols = slice(128 * head, 128 * head + 128)
        result[:, cols] = jnp.dot(
            attended, wvalue[:, cols], preferred_element_type=F32
        ).astype(BF16)
        if head % 4 == 3:
            cols = slice(128 * head - 384, 128 * head + 128)
            leaving.append(
                pltpu.make_async_copy(
                    result.at[:, cols], out_hbm.at[:, cols], load_sems.at[6 + head // 4]
                )
            )
            leaving[-1].start()
    cm.drain()
    for copy in leaving:
        copy.wait()


def on_device(hidden_in, w_down, kv_gain, queries, w_key, w_value):
    inverse = 10000.0 ** (-(np.arange(128) % 32) / 32.0)
    inverse = jnp.asarray(inverse.astype(np.float32)[None])
    vmem = pl.BlockSpec(memory_space=pltpu.VMEM)
    hbm = pl.BlockSpec(memory_space=pl.ANY)
    V = pltpu.VMEM
    return pl.pallas_call(
        body,
        out_shape=jax.ShapeDtypeStruct((TOK, HEADS * VDIM), BF16),
        in_specs=[hbm, hbm, vmem, vmem, hbm, hbm, hbm],
        out_specs=hbm,
        scratch_shapes=[
            V(hidden_in.shape, BF16),
            V(w_down.shape[::-1], BF16),
            V(queries.shape, BF16),
            V(w_key.shape, BF16),
            V(w_value.shape, BF16),
            V((TOK, HEADS * VDIM), BF16),
            V((2, 48, LAT), F32),
            V((48, LAT), F32),
            V((48, LAT), F32),
            V((48, LAT), F32),
            V((2, 4, 4, 8, 2, 16, 128), BF16),
            V((2, 4, 4, 8, 2, 16, 128), BF16),
            V((2, 8, 4, 4, 2, 16, 128), BF16),
            V((2 * EARLY, 640), BF16),
            V((2 * ROWS, 640), BF16),
            V((8, 2 * EARLY), jnp.int32),
            V((2 * ROWS, 128), jnp.int32),
            V((TOK, 128), F32),
            V((TOK, 128), F32),
            V((2, ROWS, STEP), F32),
            V((2 * ROWS, 128), F32),
            V((2 * ROWS, 128), F32),
            V((2 * ROWS, LAT), F32),
            pltpu.SemaphoreType.DMA((10,)),
            pltpu.SemaphoreType.DMA((N_SEMS,)),
            pltpu.SemaphoreType.DMA((N_SEMS,)),
        ],
        compiler_params=pltpu.CompilerParams(
            collective_id=0, has_side_effects=True, vmem_limit_bytes=56 * 2**20
        ),
        name="latent_attention",
    )(hidden_in, w_down.T, kv_gain, inverse, queries, w_key, w_value)


def solution(mesh):
    in_specs = (
        P("seq", "head"),
        P("head", None),
        P(),
        P("seq", "head"),
        P(None, "head"),
        P(None, "head"),
    )
    return jax.shard_map(
        on_device, mesh=mesh, in_specs=in_specs, out_specs=P("seq", "head"), check_vma=False
    )
```

```python
import functools

import jax
import jax.numpy as jnp
import numpy as np
from jax import lax
from jax.experimental import pallas as pl
from jax.experimental.pallas import tpu as pltpu
from jax.sharding import PartitionSpec as P

F32 = jnp.float32
BF16 = jnp.bfloat16
MESH = pl.DeviceIdType.MESH
LAT, ROPE, NOPE, VDIM = 512, 64, 128, 128
TOK, HALF, HEADS = 80, 40, 16
ROWS = HALF * HEADS
EARLY = 2560
STEP = 1280
DEEP = 896
NT = (((1,), (1,)), ((), ()))
SCALE = (NOPE + ROPE) ** (-0.5)
N_SEMS = 160


def wrap(value, size):
    return value & (size - 1)


def place():
    s = lax.axis_index("seq")
    h = lax.axis_index("head")
    return ((s >> 2) & 1) * 2 + (h >> 1), s & 3, s >> 3, h & 1


def device(x, y, z, c):
    x, y, z = wrap(x, 4), wrap(y, 4), wrap(z, 8)
    return (z * 8 + (x >> 1) * 4 + y, (x & 1) * 2 + c)


class Comm:
    def __init__(self, send_sems, recv_sems):
        self.send_sems, self.recv_sems = send_sems, recv_sems
        self.sent, self.names = [], {}

    def copy(self, name, src, dst, to):
        i = self.names.setdefault(name, len(self.names))
        return pltpu.make_async_remote_copy(
            src, dst, self.send_sems.at[i], self.recv_sems.at[i], device_id=to, device_id_type=MESH
        )

    def send(self, name, src, to, dst=None):
        copy = self.copy(name, src, src if dst is None else dst, to)
        copy.start()
        self.sent.append(copy)

    def recv(self, name, ref):
        self.copy(name, ref, ref, device(*place())).wait_recv()

    def drain(self):
        for copy in self.sent:
            copy.wait_send()
        self.sent = []


PLANE = [(dx, dy) for dx in range(4) for dy in range(4) if dx or dy]


def greet():
    x, y, z, c = place()
    bar = pltpu.get_barrier_semaphore()
    for dz in range(1, 8):
        pl.semaphore_signal(bar, 1, device_id=device(x, y, z + dz, c), device_id_type=MESH)
    for dx, dy in PLANE:
        pl.semaphore_signal(bar, 1, device_id=device(x + dx, y + dy, z, c), device_id_type=MESH)
    pl.semaphore_signal(bar, 1, device_id=device(x, y, z, 1 - c), device_id_type=MESH)


def meet():
    pl.semaphore_wait(pltpu.get_barrier_semaphore(), 7 + len(PLANE) + 1)


def gather_first(cm, kind, ref):
    x, y, z, c = place()
    if kind == "c":
        order = sorted(PLANE, key=lambda t: -(min(t[0], 4 - t[0]) + min(t[1], 4 - t[1])))
        for dx, dy in order:
            cm.send(f"cp{dx}{dy}", ref.at[c, z, x, y], device(x + dx, y + dy, z, c))
        return
    unit = ref.at[c, y, x, z] if kind == "a" else ref.at[c, x, y, z]
    for dz in (4, 3, 5, 2, 6, 1, 7):
        cm.send(f"{kind}z{dz}", unit, device(x, y, z + dz, c))


def gather_rest(cm, KA, KB, KC, arrange_a, arrange_b, arrange_c):
    x, y, z, c = place()
    sibling = device(x, y, z, 1 - c)
    other = 1 - c

    def X(d):
        return wrap(x + d, 4)

    def Y(d):
        return wrap(y + d, 4)

    def Z(d):
        return wrap(z + d, 8)

    def share(name, ref):
        cm.send("s" + name, ref, sibling)

    def col(kind, core, line, slot):
        if kind == "a":
            return KA.at[core, Y(line), X(slot)]
        return KB.at[core, X(line), Y(slot)]

    def across(kind, d):
        return device(x + d, y, z, c) if kind == "a" else device(x, y + d, z, c)

    def along(kind, d):
        return device(x, y + d, z, c) if kind == "a" else device(x + d, y, z, c)

    def start(kind):
        for dz in range(1, 8):
            unit = KA.at[c, y, x, Z(-dz)] if kind == "a" else KB.at[c, x, y, Z(-dz)]
            cm.recv(f"{kind}z{dz}", unit)
        own = col(kind, c, 0, 0)
        for d in (1, -1):
            cm.send(f"{kind}m{d}", own, across(kind, d))
        cm.send(f"{kind}m2", own, across(kind, 2))
        for d in (1, -1):
            cm.send(f"{kind}l{d}_0", own, along(kind, d))
        share(f"{kind}0_0", own)

    def middle(kind, d):
        cm.recv(f"{kind}m{d}", col(kind, c, 0, -d if d < 2 else 2))
        slot = -d if d < 2 else 2
        for e in (1, -1):
            cm.send(f"{kind}l{e}_{slot}", col(kind, c, 0, slot), along(kind, e))
        share(f"{kind}0_{slot}", col(kind, c, 0, slot))

    def last(kind, e, slot):
        cm.recv(f"{kind}l{e}_{slot}", col(kind, c, -e, slot))
        if (e == 1) == (slot in (0, 1)):
            cm.send(f"{kind}f_{slot}", col(kind, c, -e, slot), along(kind, e))
        share(f"{kind}{-e}_{slot}", col(kind, c, -e, slot))

    def far(kind, slot):
        cm.recv(f"{kind}f_{slot}", col(kind, c, 2, slot))
        share(f"{kind}2_{slot}", col(kind, c, 2, slot))

    def ring(k, part):
        rows = slice(2 * part, 2 * part + 2)
        for d in (1, -1):
            block = KC.at[c, Z(-d * k), rows]
            if k > 0:
                cm.recv(f"cz{d}_{k}_{part}", block)
            if k < 3 or (d == 1) == (part == 0):
                cm.send(f"cz{d}_{k + 1}_{part}", block, device(x, y, z + d, c))
            if k > 0:
                share(f"c{d * k}_{part}", block)

    for dx, dy in PLANE:
        cm.recv(f"cp{dx}{dy}", KC.at[c, z, X(-dx), Y(-dy)])
    ring(0, 0)
    ring(0, 1)
    share("c0", KC.at[c, z])
    start("a")
    start("b")
    ring(1, 0)
    ring(1, 1)
    for kind in "ab":
        middle(kind, 1)
    for kind in "ab":
        middle(kind, -1)
    ring(2, 0)
    ring(2, 1)
    for kind in "ab":
        last(kind, 1, 0)
    for kind in "ab":
        middle(kind, 2)
    for kind in "ab":
        last(kind, 1, 1)
    for kind in "ab":
        last(kind, -1, -1)
    ring(3, 0)
    ring(3, 1)
    for kind in "ab":
        last(kind, -1, 2)
    for kind in "ab":
        last(kind, -1, 0)
    for kind in "ab":
        last(kind, 1, -1)
    for kind in "ab":
        last(kind, -1, 1)
    for kind in "ab":
        last(kind, 1, 2)

    def line_from_sibling(kind, d):
        for slot in (0, 1, -1, 2):
            cm.recv(f"s{kind}{d}_{slot}", col(kind, other, d, slot))

    def planes_from_sibling(k):
        for part in range(2):
            cm.recv(f"sc{k}_{part}", KC.at[other, Z(-k), 2 * part : 2 * part + 2])

    line_from_sibling("a", 0)
    arrange_a(Y(0))
    cm.recv("sc0", KC.at[other, z])
    arrange_c(z)
    for k in (1, -1, 2, -2):
        planes_from_sibling(k)
    lax.fori_loop(0, 4, lambda i, carry: (arrange_c(Z(jnp.where(i < 2, i - 2, i - 1))), carry)[1], 0)
    for d in (1, -1):
        line_from_sibling("a", d)
        arrange_a(Y(d))
    for part in range(2):
        block = KC.at[c, Z(4), 2 * part : 2 * part + 2]
        cm.recv(f"cz{1 if part == 0 else -1}_4_{part}", block)
        share(f"c4_{part}", block)
    for slot in (0, 1, -1, 2):
        far("a", slot)
        far("b", slot)
    for d in (0, 1, -1):
        line_from_sibling("b", d)
    arrange_b(x >> 1)
    for k in (3, -3, 4):
        planes_from_sibling(k)
    lax.fori_loop(0, 3, lambda i, carry: (arrange_c(Z(i + 3)), carry)[1], 0)
    line_from_sibling("a", 2)
    arrange_a(Y(2))
    line_from_sibling("b", 2)
    arrange_b(1 - (x >> 1))


def lanes(shape):
    return lax.broadcasted_iota(jnp.int32, shape, 1)


def rotated(v, cos, sin):
    width = v.shape[1]
    first = (lanes(v.shape) & 63) < 32
    other = jnp.where(first, pltpu.roll(v, width - 32, 1), pltpu.roll(v, 32, 1))
    return v * cos + other * sin


def fifth(value):
    return (value * 205) >> 10


def body(
    hidden_hbm, down_hbm, gain_ref, inv_ref, queries_hbm, wkey_hbm, wvalue_hbm, out_hbm,
    hidden, down, queries, wkey, wvalue, result, part, got1, mine, got2, norm_out, norm_in, KA, KB, KC,
    keys, q, kpos, qpos, cos, sin, scores, top, total, acc,
    load_sems, send_sems, recv_sems,
):
    x, y, z, c = place()
    seq = lax.axis_index("seq")
    x_lo = x & 1
    loads = [
        pltpu.make_async_copy(src, dst, load_sems.at[i])
        for i, (src, dst) in enumerate(
            (
                (hidden_hbm, hidden),
                (down_hbm.at[:, 0:DEEP], down.at[:, 0:DEEP]),
                (down_hbm.at[:, DEEP:], down.at[:, DEEP:]),
                (queries_hbm, queries),
                (wkey_hbm, wkey),
                (wvalue_hbm, wvalue),
            )
        )
    ]
    for load in loads[:3]:
        load.start()
    greet()
    cm = Comm(send_sems, recv_sems)

    token = lax.broadcasted_iota(jnp.int32, (TOK, 128), 0)
    lane = lanes((TOK, 128))
    early_pos = seq * HALF
    late_pos = (127 - seq) * HALF
    position = jnp.where(token < HALF, early_pos + token, late_pos + token - HALF)
    angle = position.astype(F32) * inv_ref[...]
    cos[...] = jnp.cos(angle)
    sine = jnp.sin(angle)
    sin[...] = jnp.where((lane & 63) < 32, -sine, sine)

    e = lanes((8, EARLY))
    plane = fifth(e >> 6)
    r = e - 320 * plane
    in_tail = r >= 256
    slot = jnp.where(in_tail, (r - 256) >> 3, (r & 127) >> 4)
    owner = plane * 8 + (slot & 1) * 4 + (slot >> 1)
    kpos[:, 0:EARLY] = owner * HALF + jnp.where(in_tail, 32 + (r & 7), (r >> 7) * 16 + (r & 15))
    kpos[:, EARLY:] = (127 - owner) * HALF + jnp.where(
        in_tail, r & 7, 8 + (r >> 7) * 16 + (r & 15)
    )
    row = lax.broadcasted_iota(jnp.int32, (ROWS, 128), 0)
    row = row - HALF * fifth(row >> 3)
    qpos[0:ROWS] = early_pos + row
    qpos[ROWS:] = late_pos + row

    loads[0].wait()
    loads[1].wait()
    for load in loads[3:]:
        load.start()
    partial = lax.dot_general(
        hidden[:, 0:DEEP], down[:, 0:DEEP], NT, preferred_element_type=F32
    )
    loads[2].wait()
    partial = partial + lax.dot_general(
        hidden[:, DEEP:], down[:, DEEP:], NT, preferred_element_type=F32
    )
    part[0] = partial[0:48, 0:LAT]
    part[1, 0:32] = partial[48:80, 0:LAT]
    rope = jnp.concatenate([partial[:, LAT:], jnp.zeros((TOK, 128 - ROPE), F32)], 1)
    for m in range(3):
        tile = rope[32 * m : 32 * m + 16]
        if m < 2:
            tile = tile + pltpu.roll(rope[32 * m + 16 : 32 * m + 32], ROPE, 1)
        part[1, 32:48, 128 * m : 128 * m + 128] = tile
    part[1, 32:48, 384:512] = jnp.zeros((16, 128), F32)

    meet()
    tiles = [slice(16 * t, 16 * t + 16) for t in range(3)]
    order = (2, 0, 1)
    for t in order:
        cm.send(f"r1_{t}", part.at[1 - c, tiles[t]], device(x, y, z, 1 - c), got1.at[tiles[t]])
    for t in order:
        cm.recv(f"r1_{t}", got1.at[tiles[t]])
        both = part[c, tiles[t]] + got1[tiles[t]]
        mine[0, tiles[t]] = both[:, 0:256]
        mine[1, tiles[t]] = both[:, 256:512]
        norm_out[tiles[t]] = mine[x_lo, tiles[t]].astype(BF16)
        partner = (seq, (1 - x_lo) * 2 + c)
        cm.send(f"r2_{t}", mine.at[1 - x_lo, tiles[t]], partner, got2.at[tiles[t]])
        cm.send(f"r3_{t}", norm_out.at[tiles[t]], partner, norm_in.at[tiles[t]])
    gain = gain_ref[...].astype(F32).reshape(1, LAT)
    gain = jnp.where(x_lo == 0, gain[:, 0:256], gain[:, 256:512])
    cos_tiles, sin_tiles = [], []
    left = lanes((16, 128)) < 64
    for table, picked in ((cos, cos_tiles), (sin, sin_tiles)):
        for m in range(2):
            picked.append(
                jnp.where(left, table[32 * m : 32 * m + 16], table[32 * m + 16 : 32 * m + 32])
            )
        picked += [table[64:80], jnp.zeros((16, 128), F32)]
    cos_keys, sin_keys = (
        jnp.concatenate([jnp.where(x_lo == 0, p[i], p[i + 2]) for i in range(2)], 1)
        for p in (cos_tiles, sin_tiles)
    )
    for t in order:
        cm.recv(f"r2_{t}", got2.at[tiles[t]])
        cm.recv(f"r3_{t}", norm_in.at[tiles[t]])
        full = mine[x_lo, tiles[t]] + got2[tiles[t]]
        rest = mine[1 - x_lo, tiles[t]] + norm_in[tiles[t]].astype(F32)
        mean_square = jnp.sum(full * full + rest * rest, axis=1, keepdims=True) * (1.0 / LAT)
        unit = full * lax.rsqrt(mean_square + 1e-06) * gain
        if t == 2:
            unit = jnp.where(c == 1, rotated(full, cos_keys, sin_keys), unit)
        unit = unit.astype(BF16)
        for g in range(2):
            tile = unit[:, 128 * g : 128 * g + 128]
            if t == 0:
                KA[c, y, x, z, g] = tile
            elif t == 1:
                KB[c, x, y, z, g] = tile
            else:
                KC[c, z, x, y, g] = tile
        gather_first(cm, "abc"[t], (KA, KB, KC)[t])

    loads[3].wait()
    loads[4].wait()
    low = lanes((TOK, 128)) < 64
    for pair in range(HEADS // 2):
        t0, t1, t2 = (
            queries[:, 384 * pair + 128 * i : 384 * pair + 128 * i + 128] for i in range(3)
        )
        t1, t2 = t1.astype(F32), t2.astype(F32)
        second = pltpu.roll(jnp.where(low, t2, t1), 64, 1).astype(BF16)
        ropes = rotated(jnp.where(low, t1, t2), cos[...], sin[...]) * SCALE
        heads = []
        for i, nope in enumerate((t0, second)):
            head = 2 * pair + i
            lat = lax.dot_general(
                nope, wkey[:, 128 * head : 128 * head + 128], NT, preferred_element_type=F32
            )
            turned_q = jnp.where(low, pltpu.roll(ropes, 64, 1) if i else ropes, 0.0)
            heads.append(jnp.concatenate([lat * SCALE, turned_q], 1))
        for half in range(2):
            lo = half * HALF
            q[half * ROWS + TOK * pair : half * ROWS + TOK * pair + TOK] = jnp.concatenate(
                [heads[0][lo : lo + HALF], heads[1][lo : lo + HALF]], 0
            ).astype(BF16)
    top[...] = jnp.full_like(top, -1e30)
    total[...] = jnp.zeros_like(total)
    acc[...] = jnp.zeros_like(acc)


    def put(row, cols, value):
        keys[pl.ds(pl.multiple_of(row, 16), value.shape[0]), cols] = value

    def arrange_a(yy):
        def one(zz, carry):
            for xh in range(2):
                for g in range(4):
                    cols = slice(128 * g, 128 * g + 128)
                    for core in range(2):
                        row = core * EARLY + zz * 320 + 16 * (yy * 2 + xh)
                        put(row, cols, KA[core, yy, 2 * xh + g // 2, zz, g % 2])
            return carry

        lax.fori_loop(0, 8, one, 0)

    def arrange_b(xh):
        def one(zz, carry):
            for yy in range(4):
                for g in range(4):
                    cols = slice(128 * g, 128 * g + 128)
                    for core in range(2):
                        row = core * EARLY + zz * 320 + 128 + 16 * (yy * 2 + xh)
                        put(row, cols, KB[core, 2 * xh + g // 2, yy, zz, g % 2])
            return carry

        lax.fori_loop(0, 8, one, 0)

    def arrange_c(zz):
        row0 = zz * 320
        for yy in range(4):
            for xh in range(2):
                slot = yy * 2 + xh
                cols = slice(512, 640)
                packed = [KC[1, zz, 2 * xh, yy, g] for g in range(2)]
                swapped = [pltpu.roll(t.astype(F32), 64, 1).astype(BF16) for t in packed]
                put(row0 + 16 * slot, cols, packed[0])
                put(row0 + 128 + 16 * slot, cols, swapped[0])
                put(EARLY + row0 + 16 * slot, cols, swapped[1])
                put(EARLY + row0 + 128 + 16 * slot, cols, KC[1, zz, 2 * xh + 1, yy, 0])
        for yy in range(4):
            for g in range(5):
                cols = slice(128 * g, 128 * g + 128)
                if g < 4:
                    both = [KC[0, zz, 2 * xh + g // 2, yy, g % 2] for xh in range(2)]
                else:
                    both = [KC[1, zz, 2 * xh, yy, 1] for xh in range(2)]
                both = [t.astype(F32) for t in both]
                for base, lo in ((0, 0), (EARLY, 8)):
                    rows = jnp.concatenate([t[lo : lo + 8] for t in both], 0).astype(BF16)
                    put(base + row0 + 256 + 16 * yy, cols, rows)

    gather_rest(cm, KA, KB, KC, arrange_a, arrange_b, arrange_c)

    upper = z >= 4

    def offsets(i):
        fourth = jnp.where(upper, 1, 2)
        block = jnp.where(i < 2, i, jnp.where(i == 2, 0, jnp.where(i == 3, fourth, 3)))
        rows = jnp.where((i == 2) | ((i == 3) & upper), 0, ROWS)
        return pl.multiple_of(block * STEP, STEP), pl.multiple_of(rows, ROWS)

    def score(i, buffer):
        k0, q0 = offsets(i)
        s = lax.dot_general(
            q[pl.ds(q0, ROWS)], keys[pl.ds(k0, STEP)], NT, preferred_element_type=F32
        )
        limit = qpos[pl.ds(q0, ROWS)]
        allowed = kpos[0:1, pl.ds(k0, STEP)] <= jnp.concatenate([limit] * (STEP // 128), 1)
        scores[buffer] = jnp.where(allowed, s, -1e30)

    def absorb(i, buffer):
        k0, q0 = offsets(i)
        rows = pl.ds(q0, ROWS)
        s = scores[buffer]
        old = top[rows]
        new = jnp.maximum(old, jnp.max(s, axis=1, keepdims=True))
        weights = jnp.exp(s - jnp.concatenate([new] * (STEP // 128), 1))
        fade = jnp.exp(old - new)
        top[rows] = new
        total[rows] = total[rows] * fade + (
            sum(weights[:, i : i + 128] for i in range(0, STEP, 128))
        )
        product = jnp.dot(
            weights.astype(BF16), keys[pl.ds(k0, STEP), 0:LAT], preferred_element_type=F32
        )
        acc[rows] = acc[rows] * jnp.concatenate([fade] * (LAT // 128), 1) + product

    score(0, 0)

    def steps(n, carry):
        absorb(2 * n, 0)
        score(2 * n + 1, 1)
        absorb(2 * n + 1, 1)
        score(2 * n + 2, 0)
        return carry

    lax.fori_loop(0, 2, steps, 0)
    absorb(4, 0)

    loads[5].wait()
    leaving = []
    for head in range(HEADS):
        halves = []
        for half in range(2):
            rows = slice(half * ROWS + head * HALF, half * ROWS + head * HALF + HALF)
            halves.append(acc[rows] * (1.0 / jnp.sum(total[rows], axis=1, keepdims=True)))
        attended = jnp.concatenate(halves, 0).astype(BF16)
        cols = slice(128 * head, 128 * head + 128)
        result[:, cols] = jnp.dot(
            attended, wvalue[:, cols], preferred_element_type=F32
        ).astype(BF16)
        if head % 4 == 3:
            cols = slice(128 * head - 384, 128 * head + 128)
            leaving.append(
                pltpu.make_async_copy(
                    result.at[:, cols], out_hbm.at[:, cols], load_sems.at[6 + head // 4]
                )
            )
            leaving[-1].start()
    cm.drain()
    for copy in leaving:
        copy.wait()


def on_device(hidden_in, w_down, kv_gain, queries, w_key, w_value):
    inverse = 10000.0 ** (-(np.arange(128) % 32) / 32.0)
    inverse = jnp.asarray(inverse.astype(np.float32)[None])
    vmem = pl.BlockSpec(memory_space=pltpu.VMEM)
    hbm = pl.BlockSpec(memory_space=pl.ANY)
    V = pltpu.VMEM
    return pl.pallas_call(
        body,
        out_shape=jax.ShapeDtypeStruct((TOK, HEADS * VDIM), BF16),
        in_specs=[hbm, hbm, vmem, vmem, hbm, hbm, hbm],
        out_specs=hbm,
        scratch_shapes=[
            V(hidden_in.shape, BF16),
            V(w_down.shape[::-1], BF16),
            V(queries.shape, BF16),
            V(w_key.shape, BF16),
            V(w_value.shape, BF16),
            V((TOK, HEADS * VDIM), BF16),
            V((2, 48, LAT), F32),
            V((48, LAT), F32),
            V((2, 48, 256), F32),
            V((48, 256), F32),
            V((48, 256), BF16),
            V((48, 256), BF16),
            V((2, 4, 4, 8, 2, 16, 128), BF16),
            V((2, 4, 4, 8, 2, 16, 128), BF16),
            V((2, 8, 4, 4, 2, 16, 128), BF16),
            V((2 * EARLY, 640), BF16),
            V((2 * ROWS, 640), BF16),
            V((8, 2 * EARLY), jnp.int32),
            V((2 * ROWS, 128), jnp.int32),
            V((TOK, 128), F32),
            V((TOK, 128), F32),
            V((2, ROWS, STEP), F32),
            V((2 * ROWS, 128), F32),
            V((2 * ROWS, 128), F32),
            V((2 * ROWS, LAT), F32),
            pltpu.SemaphoreType.DMA((10,)),
            pltpu.SemaphoreType.DMA((N_SEMS,)),
            pltpu.SemaphoreType.DMA((N_SEMS,)),
        ],
        compiler_params=pltpu.CompilerParams(
            collective_id=0, has_side_effects=True, vmem_limit_bytes=56 * 2**20
        ),
        name="latent_attention",
    )(hidden_in, w_down.T, kv_gain, inverse, queries, w_key, w_value)


def solution(mesh):
    in_specs = (
        P("seq", "head"),
        P("head", None),
        P(),
        P("seq", "head"),
        P(None, "head"),
        P(None, "head"),
    )
    return jax.shard_map(
        on_device, mesh=mesh, in_specs=in_specs, out_specs=P("seq", "head"), check_vma=False
    )
```

```python
import functools

import jax
import jax.numpy as jnp
import numpy as np
from jax import lax
from jax.experimental import pallas as pl
from jax.experimental.pallas import tpu as pltpu
from jax.sharding import PartitionSpec as P

F32 = jnp.float32
BF16 = jnp.bfloat16
MESH = pl.DeviceIdType.MESH
LAT, ROPE, NOPE, VDIM = 512, 64, 128, 128
TOK, HALF, HEADS = 80, 40, 16
ROWS = HALF * HEADS
EARLY = 2560
STEP = 1280
DEEP = 896
NT = (((1,), (1,)), ((), ()))
SCALE = (NOPE + ROPE) ** (-0.5)
N_SEMS = 160


def wrap(value, size):
    return value & (size - 1)


def place():
    s = lax.axis_index("seq")
    h = lax.axis_index("head")
    return ((s >> 2) & 1) * 2 + (h >> 1), s & 3, s >> 3, h & 1


def device(x, y, z, c):
    x, y, z = wrap(x, 4), wrap(y, 4), wrap(z, 8)
    return (z * 8 + (x >> 1) * 4 + y, (x & 1) * 2 + c)


class Comm:
    def __init__(self, send_sems, recv_sems):
        self.send_sems, self.recv_sems = send_sems, recv_sems
        self.sent, self.names = [], {}

    def copy(self, name, src, dst, to):
        i = self.names.setdefault(name, len(self.names))
        return pltpu.make_async_remote_copy(
            src, dst, self.send_sems.at[i], self.recv_sems.at[i], device_id=to, device_id_type=MESH
        )

    def send(self, name, src, to, dst=None):
        copy = self.copy(name, src, src if dst is None else dst, to)
        copy.start()
        self.sent.append(copy)

    def recv(self, name, ref):
        self.copy(name, ref, ref, device(*place())).wait_recv()

    def drain(self):
        for copy in self.sent:
            copy.wait_send()
        self.sent = []


PLANE = [(dx, dy) for dx in range(4) for dy in range(4) if dx or dy]


def greet():
    x, y, z, c = place()
    bar = pltpu.get_barrier_semaphore()
    for dz in range(1, 8):
        pl.semaphore_signal(bar, 1, device_id=device(x, y, z + dz, c), device_id_type=MESH)
    for dx, dy in PLANE:
        pl.semaphore_signal(bar, 1, device_id=device(x + dx, y + dy, z, c), device_id_type=MESH)
    pl.semaphore_signal(bar, 1, device_id=device(x, y, z, 1 - c), device_id_type=MESH)


def meet():
    pl.semaphore_wait(pltpu.get_barrier_semaphore(), 7 + len(PLANE) + 1)


def gather_first(cm, kind, ref):
    x, y, z, c = place()
    if kind == "c":
        order = sorted(PLANE, key=lambda t: -(min(t[0], 4 - t[0]) + min(t[1], 4 - t[1])))
        for dx, dy in order:
            cm.send(f"cp{dx}{dy}", ref.at[c, z, x, y], device(x + dx, y + dy, z, c))
        return
    unit = ref.at[c, y, x, z] if kind == "a" else ref.at[c, x, y, z]
    for dz in (4, 3, 5, 2, 6, 1, 7):
        cm.send(f"{kind}z{dz}", unit, device(x, y, z + dz, c))


def gather_rest(cm, KA, KB, KC, arrange_a, arrange_b, arrange_c):
    x, y, z, c = place()
    sibling = device(x, y, z, 1 - c)
    other = 1 - c

    def X(d):
        return wrap(x + d, 4)

    def Y(d):
        return wrap(y + d, 4)

    def Z(d):
        return wrap(z + d, 8)

    def share(name, ref):
        cm.send("s" + name, ref, sibling)

    def col(kind, core, line, slot):
        if kind == "a":
            return KA.at[core, Y(line), X(slot)]
        return KB.at[core, X(line), Y(slot)]

    def across(kind, d):
        return device(x + d, y, z, c) if kind == "a" else device(x, y + d, z, c)

    def along(kind, d):
        return device(x, y + d, z, c) if kind == "a" else device(x + d, y, z, c)

    def start(kind):
        for dz in range(1, 8):
            unit = KA.at[c, y, x, Z(-dz)] if kind == "a" else KB.at[c, x, y, Z(-dz)]
            cm.recv(f"{kind}z{dz}", unit)
        own = col(kind, c, 0, 0)
        for d in (1, -1):
            cm.send(f"{kind}m{d}", own, across(kind, d))
        cm.send(f"{kind}m2", own, across(kind, 2))
        for d in (1, -1):
            cm.send(f"{kind}l{d}_0", own, along(kind, d))
        share(f"{kind}0_0", own)

    def middle(kind, d):
        cm.recv(f"{kind}m{d}", col(kind, c, 0, -d if d < 2 else 2))
        slot = -d if d < 2 else 2
        for e in (1, -1):
            cm.send(f"{kind}l{e}_{slot}", col(kind, c, 0, slot), along(kind, e))
        share(f"{kind}0_{slot}", col(kind, c, 0, slot))

    def last(kind, e, slot):
        cm.recv(f"{kind}l{e}_{slot}", col(kind, c, -e, slot))
        if (e == 1) == (slot in (0, 1)):
            cm.send(f"{kind}f_{slot}", col(kind, c, -e, slot), along(kind, e))
        share(f"{kind}{-e}_{slot}", col(kind, c, -e, slot))

    def far(kind, slot):
        cm.recv(f"{kind}f_{slot}", col(kind, c, 2, slot))
        share(f"{kind}2_{slot}", col(kind, c, 2, slot))

    def ring(k, part):
        rows = slice(2 * part, 2 * part + 2)
        for d in (1, -1):
            block = KC.at[c, Z(-d * k), rows]
            if k > 0:
                cm.recv(f"cz{d}_{k}_{part}", block)
            if k < 3 or (d == 1) == (part == 0):
                cm.send(f"cz{d}_{k + 1}_{part}", block, device(x, y, z + d, c))
            if k > 0:
                share(f"c{d * k}_{part}", block)

    for dx, dy in PLANE:
        cm.recv(f"cp{dx}{dy}", KC.at[c, z, X(-dx), Y(-dy)])
    ring(0, 0)
    ring(0, 1)
    share("c0", KC.at[c, z])
    start("a")
    start("b")
    ring(1, 0)
    ring(1, 1)
    for kind in "ab":
        middle(kind, 1)
    for kind in "ab":
        middle(kind, -1)
    ring(2, 0)
    ring(2, 1)
    for kind in "ab":
        last(kind, 1, 0)
    for kind in "ab":
        middle(kind, 2)
    for kind in "ab":
        last(kind, 1, 1)
    for kind in "ab":
        last(kind, -1, -1)
    ring(3, 0)
    ring(3, 1)
    for kind in "ab":
        last(kind, -1, 2)
    for kind in "ab":
        last(kind, -1, 0)
    for kind in "ab":
        last(kind, 1, -1)
    for kind in "ab":
        last(kind, -1, 1)
    for kind in "ab":
        last(kind, 1, 2)

    def line_from_sibling(kind, d):
        for slot in (0, 1, -1, 2):
            cm.recv(f"s{kind}{d}_{slot}", col(kind, other, d, slot))

    def planes_from_sibling(k):
        for part in range(2):
            cm.recv(f"sc{k}_{part}", KC.at[other, Z(-k), 2 * part : 2 * part + 2])

    line_from_sibling("a", 0)
    arrange_a(Y(0))
    cm.recv("sc0", KC.at[other, z])
    arrange_c(z)
    for k in (1, -1, 2, -2):
        planes_from_sibling(k)
    lax.fori_loop(0, 4, lambda i, carry: (arrange_c(Z(jnp.where(i < 2, i - 2, i - 1))), carry)[1], 0)
    for d in (1, -1):
        line_from_sibling("a", d)
        arrange_a(Y(d))
    for part in range(2):
        block = KC.at[c, Z(4), 2 * part : 2 * part + 2]
        cm.recv(f"cz{1 if part == 0 else -1}_4_{part}", block)
        share(f"c4_{part}", block)
    for slot in (0, 1, -1, 2):
        far("a", slot)
        far("b", slot)
    for d in (0, 1, -1):
        line_from_sibling("b", d)
    arrange_b(x >> 1)
    for k in (3, -3, 4):
        planes_from_sibling(k)
    lax.fori_loop(0, 3, lambda i, carry: (arrange_c(Z(i + 3)), carry)[1], 0)
    line_from_sibling("a", 2)
    arrange_a(Y(2))
    line_from_sibling("b", 2)
    arrange_b(1 - (x >> 1))


def lanes(shape):
    return lax.broadcasted_iota(jnp.int32, shape, 1)


def rotated(v, cos, sin):
    width = v.shape[1]
    first = (lanes(v.shape) & 63) < 32
    other = jnp.where(first, pltpu.roll(v, width - 32, 1), pltpu.roll(v, 32, 1))
    return v * cos + other * sin


def fifth(value):
    return (value * 205) >> 10


def body(
    hidden_hbm, down_hbm, gain_ref, inv_ref, queries_hbm, wkey_hbm, wvalue_hbm, out_hbm,
    hidden, down, queries, wkey, wvalue, result, part, got1, mine, got2, norm_out, norm_in, KA, KB, KC,
    keys, q, kpos, qpos, cos, sin, scores, top, total, acc,
    load_sems, send_sems, recv_sems,
):
    x, y, z, c = place()
    seq = lax.axis_index("seq")
    x_lo = x & 1
    loads = [
        pltpu.make_async_copy(src, dst, load_sems.at[i])
        for i, (src, dst) in enumerate(
            (
                (hidden_hbm, hidden),
                (down_hbm.at[:, 0:DEEP], down.at[:, 0:DEEP]),
                (down_hbm.at[:, DEEP:], down.at[:, DEEP:]),
                (queries_hbm, queries),
                (wkey_hbm, wkey),
                (wvalue_hbm, wvalue),
            )
        )
    ]
    for load in loads[:3]:
        load.start()
    greet()
    cm = Comm(send_sems, recv_sems)

    token = lax.broadcasted_iota(jnp.int32, (TOK, 128), 0)
    lane = lanes((TOK, 128))
    early_pos = seq * HALF
    late_pos = (127 - seq) * HALF
    position = jnp.where(token < HALF, early_pos + token, late_pos + token - HALF)
    angle = position.astype(F32) * inv_ref[...]
    cos[...] = jnp.cos(angle)
    sine = jnp.sin(angle)
    sin[...] = jnp.where((lane & 63) < 32, -sine, sine)

    e = lanes((8, EARLY))
    plane = fifth(e >> 6)
    r = e - 320 * plane
    in_tail = r >= 256
    slot = jnp.where(in_tail, (r - 256) >> 3, (r & 127) >> 4)
    owner = plane * 8 + (slot & 1) * 4 + (slot >> 1)
    kpos[:, 0:EARLY] = owner * HALF + jnp.where(in_tail, 32 + (r & 7), (r >> 7) * 16 + (r & 15))
    kpos[:, EARLY:] = (127 - owner) * HALF + jnp.where(
        in_tail, r & 7, 8 + (r >> 7) * 16 + (r & 15)
    )
    row = lax.broadcasted_iota(jnp.int32, (ROWS, 128), 0)
    row = row - HALF * fifth(row >> 3)
    qpos[0:ROWS] = early_pos + row
    qpos[ROWS:] = late_pos + row

    loads[0].wait()
    loads[1].wait()
    for load in loads[3:]:
        load.start()
    partial = lax.dot_general(
        hidden[:, 0:DEEP], down[:, 0:DEEP], NT, preferred_element_type=F32
    )
    loads[2].wait()
    partial = partial + lax.dot_general(
        hidden[:, DEEP:], down[:, DEEP:], NT, preferred_element_type=F32
    )
    part[0] = partial[0:48, 0:LAT]
    part[1, 0:32] = partial[48:80, 0:LAT]
    rope = jnp.concatenate([partial[:, LAT:], jnp.zeros((TOK, 128 - ROPE), F32)], 1)
    for m in range(3):
        tile = rope[32 * m : 32 * m + 16]
        if m < 2:
            tile = tile + pltpu.roll(rope[32 * m + 16 : 32 * m + 32], ROPE, 1)
        part[1, 32:48, 128 * m : 128 * m + 128] = tile
    part[1, 32:48, 384:512] = jnp.zeros((16, 128), F32)

    meet()
    tiles = [slice(16 * t, 16 * t + 16) for t in range(3)]
    order = (2, 0, 1)
    cm.send("r1", part.at[1 - c], device(x, y, z, 1 - c), got1)
    cm.recv("r1", got1)
    for t in order:
        both = part[c, tiles[t]] + got1[tiles[t]]
        mine[0, tiles[t]] = both[:, 0:256]
        mine[1, tiles[t]] = both[:, 256:512]
        norm_out[tiles[t]] = mine[x_lo, tiles[t]].astype(BF16)
        partner = (seq, (1 - x_lo) * 2 + c)
        cm.send(f"r2_{t}", mine.at[1 - x_lo, tiles[t]], partner, got2.at[tiles[t]])
        cm.send(f"r3_{t}", norm_out.at[tiles[t]], partner, norm_in.at[tiles[t]])
    gain = gain_ref[...].astype(F32).reshape(1, LAT)
    gain = jnp.where(x_lo == 0, gain[:, 0:256], gain[:, 256:512])
    cos_tiles, sin_tiles = [], []
    left = lanes((16, 128)) < 64
    for table, picked in ((cos, cos_tiles), (sin, sin_tiles)):
        for m in range(2):
            picked.append(
                jnp.where(left, table[32 * m : 32 * m + 16], table[32 * m + 16 : 32 * m + 32])
            )
        picked += [table[64:80], jnp.zeros((16, 128), F32)]
    cos_keys, sin_keys = (
        jnp.concatenate([jnp.where(x_lo == 0, p[i], p[i + 2]) for i in range(2)], 1)
        for p in (cos_tiles, sin_tiles)
    )
    for t in order:
        cm.recv(f"r2_{t}", got2.at[tiles[t]])
        cm.recv(f"r3_{t}", norm_in.at[tiles[t]])
        full = mine[x_lo, tiles[t]] + got2[tiles[t]]
        rest = mine[1 - x_lo, tiles[t]] + norm_in[tiles[t]].astype(F32)
        mean_square = jnp.sum(full * full + rest * rest, axis=1, keepdims=True) * (1.0 / LAT)
        unit = full * lax.rsqrt(mean_square + 1e-06) * gain
        if t == 2:
            unit = jnp.where(c == 1, rotated(full, cos_keys, sin_keys), unit)
        unit = unit.astype(BF16)
        for g in range(2):
            tile = unit[:, 128 * g : 128 * g + 128]
            if t == 0:
                KA[c, y, x, z, g] = tile
            elif t == 1:
                KB[c, x, y, z, g] = tile
            else:
                KC[c, z, x, y, g] = tile
        gather_first(cm, "abc"[t], (KA, KB, KC)[t])

    loads[3].wait()
    loads[4].wait()
    low = lanes((TOK, 128)) < 64
    for pair in range(HEADS // 2):
        t0, t1, t2 = (
            queries[:, 384 * pair + 128 * i : 384 * pair + 128 * i + 128] for i in range(3)
        )
        t1, t2 = t1.astype(F32), t2.astype(F32)
        second = pltpu.roll(jnp.where(low, t2, t1), 64, 1).astype(BF16)
        ropes = rotated(jnp.where(low, t1, t2), cos[...], sin[...]) * SCALE
        heads = []
        for i, nope in enumerate((t0, second)):
            head = 2 * pair + i
            lat = lax.dot_general(
                nope, wkey[:, 128 * head : 128 * head + 128], NT, preferred_element_type=F32
            )
            turned_q = jnp.where(low, pltpu.roll(ropes, 64, 1) if i else ropes, 0.0)
            heads.append(jnp.concatenate([lat * SCALE, turned_q], 1))
        for half in range(2):
            lo = half * HALF
            q[half * ROWS + TOK * pair : half * ROWS + TOK * pair + TOK] = jnp.concatenate(
                [heads[0][lo : lo + HALF], heads[1][lo : lo + HALF]], 0
            ).astype(BF16)
    top[...] = jnp.full_like(top, -1e30)
    total[...] = jnp.zeros_like(total)
    acc[...] = jnp.zeros_like(acc)


    def put(row, cols, value):
        keys[pl.ds(pl.multiple_of(row, 16), value.shape[0]), cols] = value

    def arrange_a(yy):
        def one(zz, carry):
            for xh in range(2):
                for g in range(4):
                    cols = slice(128 * g, 128 * g + 128)
                    for core in range(2):
                        row = core * EARLY + zz * 320 + 16 * (yy * 2 + xh)
                        put(row, cols, KA[core, yy, 2 * xh + g // 2, zz, g % 2])
            return carry

        lax.fori_loop(0, 8, one, 0)

    def arrange_b(xh):
        def one(zz, carry):
            for yy in range(4):
                for g in range(4):
                    cols = slice(128 * g, 128 * g + 128)
                    for core in range(2):
                        row = core * EARLY + zz * 320 + 128 + 16 * (yy * 2 + xh)
                        put(row, cols, KB[core, 2 * xh + g // 2, yy, zz, g % 2])
            return carry

        lax.fori_loop(0, 8, one, 0)

    def arrange_c(zz):
        row0 = zz * 320
        for yy in range(4):
            for xh in range(2):
                slot = yy * 2 + xh
                cols = slice(512, 640)
                packed = [KC[1, zz, 2 * xh, yy, g] for g in range(2)]
                swapped = [pltpu.roll(t.astype(F32), 64, 1).astype(BF16) for t in packed]
                put(row0 + 16 * slot, cols, packed[0])
                put(row0 + 128 + 16 * slot, cols, swapped[0])
                put(EARLY + row0 + 16 * slot, cols, swapped[1])
                put(EARLY + row0 + 128 + 16 * slot, cols, KC[1, zz, 2 * xh + 1, yy, 0])
        for yy in range(4):
            for g in range(5):
                cols = slice(128 * g, 128 * g + 128)
                if g < 4:
                    both = [KC[0, zz, 2 * xh + g // 2, yy, g % 2] for xh in range(2)]
                else:
                    both = [KC[1, zz, 2 * xh, yy, 1] for xh in range(2)]
                both = [t.astype(F32) for t in both]
                for base, lo in ((0, 0), (EARLY, 8)):
                    rows = jnp.concatenate([t[lo : lo + 8] for t in both], 0).astype(BF16)
                    put(base + row0 + 256 + 16 * yy, cols, rows)

    gather_rest(cm, KA, KB, KC, arrange_a, arrange_b, arrange_c)

    upper = z >= 4

    def offsets(i):
        fourth = jnp.where(upper, 1, 2)
        block = jnp.where(i < 2, i, jnp.where(i == 2, 0, jnp.where(i == 3, fourth, 3)))
        rows = jnp.where((i == 2) | ((i == 3) & upper), 0, ROWS)
        return pl.multiple_of(block * STEP, STEP), pl.multiple_of(rows, ROWS)

    def score(i, buffer):
        k0, q0 = offsets(i)
        s = lax.dot_general(
            q[pl.ds(q0, ROWS)], keys[pl.ds(k0, STEP)], NT, preferred_element_type=F32
        )
        limit = qpos[pl.ds(q0, ROWS)]
        allowed = kpos[0:1, pl.ds(k0, STEP)] <= jnp.concatenate([limit] * (STEP // 128), 1)
        scores[buffer] = jnp.where(allowed, s, -1e30)

    def absorb(i, buffer):
        k0, q0 = offsets(i)
        rows = pl.ds(q0, ROWS)
        s = scores[buffer]
        old = top[rows]
        new = jnp.maximum(old, jnp.max(s, axis=1, keepdims=True))
        weights = jnp.exp(s - jnp.concatenate([new] * (STEP // 128), 1))
        fade = jnp.exp(old - new)
        top[rows] = new
        total[rows] = total[rows] * fade + (
            sum(weights[:, i : i + 128] for i in range(0, STEP, 128))
        )
        product = jnp.dot(
            weights.astype(BF16), keys[pl.ds(k0, STEP), 0:LAT], preferred_element_type=F32
        )
        acc[rows] = acc[rows] * jnp.concatenate([fade] * (LAT // 128), 1) + product

    score(0, 0)

    def steps(n, carry):
        absorb(2 * n, 0)
        score(2 * n + 1, 1)
        absorb(2 * n + 1, 1)
        score(2 * n + 2, 0)
        return carry

    lax.fori_loop(0, 2, steps, 0)
    absorb(4, 0)

    loads[5].wait()
    leaving = []
    for head in range(HEADS):
        halves = []
        for half in range(2):
            rows = slice(half * ROWS + head * HALF, half * ROWS + head * HALF + HALF)
            halves.append(acc[rows] * (1.0 / jnp.sum(total[rows], axis=1, keepdims=True)))
        attended = jnp.concatenate(halves, 0).astype(BF16)
        cols = slice(128 * head, 128 * head + 128)
        result[:, cols] = jnp.dot(
            attended, wvalue[:, cols], preferred_element_type=F32
        ).astype(BF16)
        if head % 4 == 3:
            cols = slice(128 * head - 384, 128 * head + 128)
            leaving.append(
                pltpu.make_async_copy(
                    result.at[:, cols], out_hbm.at[:, cols], load_sems.at[6 + head // 4]
                )
            )
            leaving[-1].start()
    cm.drain()
    for copy in leaving:
        copy.wait()


def on_device(hidden_in, w_down, kv_gain, queries, w_key, w_value):
    inverse = 10000.0 ** (-(np.arange(128) % 32) / 32.0)
    inverse = jnp.asarray(inverse.astype(np.float32)[None])
    vmem = pl.BlockSpec(memory_space=pltpu.VMEM)
    hbm = pl.BlockSpec(memory_space=pl.ANY)
    V = pltpu.VMEM
    return pl.pallas_call(
        body,
        out_shape=jax.ShapeDtypeStruct((TOK, HEADS * VDIM), BF16),
        in_specs=[hbm, hbm, vmem, vmem, hbm, hbm, hbm],
        out_specs=hbm,
        scratch_shapes=[
            V(hidden_in.shape, BF16),
            V(w_down.shape[::-1], BF16),
            V(queries.shape, BF16),
            V(w_key.shape, BF16),
            V(w_value.shape, BF16),
            V((TOK, HEADS * VDIM), BF16),
            V((2, 48, LAT), F32),
            V((48, LAT), F32),
            V((2, 48, 256), F32),
            V((48, 256), F32),
            V((48, 256), BF16),
            V((48, 256), BF16),
            V((2, 4, 4, 8, 2, 16, 128), BF16),
            V((2, 4, 4, 8, 2, 16, 128), BF16),
            V((2, 8, 4, 4, 2, 16, 128), BF16),
            V((2 * EARLY, 640), BF16),
            V((2 * ROWS, 640), BF16),
            V((8, 2 * EARLY), jnp.int32),
            V((2 * ROWS, 128), jnp.int32),
            V((TOK, 128), F32),
            V((TOK, 128), F32),
            V((2, ROWS, STEP), F32),
            V((2 * ROWS, 128), F32),
            V((2 * ROWS, 128), F32),
            V((2 * ROWS, LAT), F32),
            pltpu.SemaphoreType.DMA((10,)),
            pltpu.SemaphoreType.DMA((N_SEMS,)),
            pltpu.SemaphoreType.DMA((N_SEMS,)),
        ],
        compiler_params=pltpu.CompilerParams(
            collective_id=0, has_side_effects=True, vmem_limit_bytes=56 * 2**20
        ),
        name="latent_attention",
    )(hidden_in, w_down.T, kv_gain, inverse, queries, w_key, w_value)


def solution(mesh):
    in_specs = (
        P("seq", "head"),
        P("head", None),
        P(),
        P("seq", "head"),
        P(None, "head"),
        P(None, "head"),
    )
    return jax.shard_map(
        on_device, mesh=mesh, in_specs=in_specs, out_specs=P("seq", "head"), check_vma=False
    )
```
